768 devices in a mesh: dp: 96 (over y, z), fsdp: 8 (over x, core).
Axes of the slice: x: 4, y: 8, z: 12, core: 2. Of those that a mesh axis runs over, the one named last changes fastest.
Arguments:
- tokens: bfloat16 [98304, 4096], P(('dp', 'fsdp')), may hold values from -6 to 6
- value_grad: bfloat16 [98304, 1024], P(('dp', 'fsdp')), may hold values from -6 to 6
- value_weight: bfloat16 [4096, 1024], P('fsdp'), may hold values from -0.1875 to 0.1875
- counts: int32 [768], P(('dp', 'fsdp')), may hold values from 66 to 88, as said below
- chosen_rows: int32 [768, 88], P(('dp', 'fsdp')), may hold values from 0 to 127, as said below
- loss_scale: float32 [1], replicated, may hold values from 129.98462 to 519.9385
Outputs:
- grad_tokens: bfloat16 [98304, 4096], P(('dp', 'fsdp'))
- grad_weight: float32 [4096, 1024], P('fsdp')
The draws below stay inside these ranges and needn't reach their ends.
Inputs may be any that keep to these rules, and one draw needn't show every extreme that they name: `counts`: each device's count lies between 66 and 88; some device has exactly 88, a different one in different draws. `chosen_rows`: the 88 entries of a device's row are distinct row numbers of that device.
All inputs are finite; a program needn't handle non-finite values.
Results may differ from the reference program's by a relative error of at most 0.001.
Values may be sent and summed in bfloat16 or wider, within the bound.
A program may use at most 32 MiB of HBM per device.

```python
import math
import jax
import jax.numpy as jnp
from jax import lax

D = 4096
KV = 1024
ROWS_DEV = 128
SEL_MAX = 88
SHARDS = 768
TOKENS = 98304


def draw_counts(key, part):
    values = jax.random.randint(key, (SHARDS,), SEL_MAX * 3 // 4, SEL_MAX + 1)
    fullest = jax.random.randint(jax.random.fold_in(key, 7), (), 0, SHARDS)
    values = jnp.where(jnp.arange(SHARDS) == fullest, SEL_MAX, values)
    return values.astype(jnp.int32)


def draw_chosen_rows(key, part):
    keys = jax.random.split(jax.random.fold_in(key, 11), SHARDS)

    def one_device(device_key):
        return jax.random.permutation(device_key, ROWS_DEV)[:SEL_MAX]
    return jax.vmap(one_device)(keys).astype(jnp.int32)


def level_of(stream_key, extent, pieces, low, largest):
    def one(axis_at, blocks):
        steps = jax.random.uniform(jax.random.fold_in(jax.random.fold_in(stream_key, 6), axis_at), (blocks,), jnp.float32, low / len(pieces), largest / len(pieces))
        return jnp.repeat(jnp.exp(steps), extent[axis_at] // blocks).reshape((-1,) + (1,) * (len(extent) - axis_at - 1))

    loudness = one(*pieces[0])
    for cut in pieces[1:]:
        loudness = loudness * one(*cut)
    return loudness


def bell_draw(rng, shape, scale, reach, cuts=(), kind=jnp.bfloat16):
    level = level_of(rng, shape, cuts, -0.22, 0.18) if cuts else 1.0
    values = jax.random.normal(rng, shape, jnp.float32) * scale * level
    return jnp.minimum(jnp.maximum(values, -reach), reach).astype(kind)


def setup_inputs(seed: int = 0) -> dict:
    key_of = jax.random.split(jax.random.key(seed), 7)
    tokens = bell_draw(key_of[0], (TOKENS, D), 1.0, 6.0, ((0, 768),))
    value_grad = bell_draw(key_of[1], (TOKENS, KV), 1.0, 6.0, ((0, 768),))
    value_weight = bell_draw(key_of[2], (D, KV), KV ** -0.5, 0.1875, ((0, 8),))
    counts = draw_counts(jax.random.fold_in(key_of[6], 71), 0)
    chosen_rows = draw_chosen_rows(jax.random.fold_in(key_of[6], 71), 0)
    loss_scale = jnp.clip(jnp.exp(jax.random.uniform(key_of[5], (1,), jnp.float32, math.log(129.98462), math.log(519.9385))), 129.98462, 519.9385)
    return {"tokens": tokens, "value_grad": value_grad, "value_weight": value_weight, "counts": counts, "chosen_rows": chosen_rows, "loss_scale": loss_scale}


def reference(tokens, value_grad, value_weight, counts, chosen_rows, loss_scale):
    blocks = tokens.reshape(SHARDS, ROWS_DEV, D)
    grads = value_grad.reshape(SHARDS, ROWS_DEV, KV)
    slots = jnp.arange(SEL_MAX, dtype=jnp.int32)

    def one_device(carry, item):
        block, grad_block, count, chosen = item
        live_mask = (slots < count)[:, None]
        picked = block[chosen]
        cotangent = jnp.where(live_mask, grad_block[chosen], jnp.zeros((), jnp.bfloat16)).astype(jnp.bfloat16)
        carry = carry + jnp.dot(picked.T, cotangent, preferred_element_type=jnp.float32)
        slot_grad = jnp.dot(cotangent, value_weight.T, preferred_element_type=jnp.float32).astype(jnp.bfloat16)
        placed = jnp.zeros((ROWS_DEV, D), jnp.bfloat16).at[chosen].set(slot_grad)
        return carry, placed

    start = jnp.zeros((D, KV), jnp.float32)
    total, placed_all = lax.scan(one_device, start, (blocks, grads, counts, chosen_rows))
    return placed_all.reshape(TOKENS, D), total / loss_scale[0]
```

```python
import jax
import jax.numpy as jnp
from jax import lax
from jax.experimental import pallas as pl
from jax.experimental.pallas import tpu as pltpu
from jax.sharding import PartitionSpec as P

MESH = pl.DeviceIdType.MESH
NY, NZ, NF = 8, 12, 8
SLOTS = 96
ROWS, D, KV = 128, 4096, 1024
W = D // NF
CH = 4
CW = W // CH
ZR = 48
LANE = KV // NY
LONG, SHORT = NY // 2, NY // 2 - 1
f32, bf16 = jnp.float32, jnp.bfloat16


def dot(a, b, ca, cb):
    return lax.dot_general(a, b, (((ca,), (cb,)), ((), ())), preferred_element_type=f32)


def kernel(
    tok, vg, wt, sel, scale, gt_out, gw_out,
    picked, cots, parts, slot, own, gt, part, rl, rs, red, zrecv, zsum, full,
    cot_s, cot_r, sib_s, sib_r, pk_s, pk_r, sg_s, sg_r,
    l_s, l_r, s_s, s_r, z_s, z_r, az_s, az_r, al_s, al_r, as_s, as_r, out_s,
):
    dp, fs = lax.axis_index("dp"), lax.axis_index("fsdp")
    y, z = dp // NZ, lax.rem(dp, NZ)
    c, x = lax.rem(fs, 2), fs // 2
    sgn = 1 - 2 * c
    sib = x * 2 + 1 - c

    def at_y(v):
        return lax.rem(v + 2 * NY, NY)

    y_up, y_dn = at_y(y + sgn) * NZ + z, at_y(y - sgn) * NZ + z

    def zdev(d):
        return lax.rem(z + d, NZ)

    def fdev(d):
        return lax.rem(fs + d, NF)

    def xdev(d):
        return lax.rem(x + d, 4) * 2 + c

    def rcopy(src, dst, ss, rs_, dev):
        return pltpu.make_async_remote_copy(
            src_ref=src, dst_ref=dst, send_sem=ss, recv_sem=rs_, device_id=dev, device_id_type=MESH
        )

    barrier = pltpu.get_barrier_semaphore()
    peers = [(dp, fdev(d)) for d in range(1, NF)]
    peers += [(y_up, fs), (y_dn, fs)]
    peers += [(y * NZ + zdev(d), fs) for d in range(1, NZ)]
    for peer in peers:
        pl.semaphore_signal(barrier, inc=1, device_id=peer, device_id_type=MESH)

    rows = lax.broadcasted_iota(jnp.int32, (ROWS, ROWS), 0)
    hot = jnp.where(rows == sel[0:1, :], 1.0, 0.0).astype(bf16)
    cots[fs] = dot(hot, vg[...], 0, 0)[:SLOTS].astype(bf16)
    pl.semaphore_wait(barrier, len(peers))

    sends = []

    def go(cp):
        cp.start()
        sends.append(cp)

    for d in (1, 3, 2):
        go(rcopy(cots.at[fs], cots.at[fs], cot_s.at[d - 1], cot_r.at[d - 1], (dp, xdev(d))))
    go(rcopy(cots.at[fs], cots.at[fs], sib_s.at[0], sib_r.at[0], (dp, sib)))

    for b in range(4):
        cols = slice(b * 1024, (b + 1) * 1024)
        picked[:, cols] = dot(hot, tok[:, cols], 0, 0)[:SLOTS].astype(bf16)
    for k in range(CH):
        for d in (2, 6, 3, 7, 4, 5, 1):
            to = fdev(d)
            cols = pl.ds(pl.multiple_of(to * W + k * CW, CW), CW)
            go(rcopy(picked.at[:, cols], parts.at[k, fs], pk_s.at[k, d - 1], pk_r.at[k, d - 1], (dp, to)))
        cols = pl.ds(pl.multiple_of(fs * W + k * CW, CW), CW)
        parts[k, fs] = picked[:, cols]

    for d in (1, 3, 2):
        frm = xdev(4 - d)
        rcopy(cots.at[frm], cots.at[frm], cot_s.at[d - 1], cot_r.at[d - 1], (dp, frm)).wait_recv()
        go(rcopy(cots.at[frm], cots.at[frm], sib_s.at[d], sib_r.at[d], (dp, sib)))
    for d in range(4):
        frm = lax.rem(x + 4 - d, 4) * 2 + 1 - c
        rcopy(cots.at[frm], cots.at[frm], sib_s.at[d], sib_r.at[d], (dp, sib)).wait_recv()

    def long_copy(k, s):
        j = at_y(y - sgn * (LONG - s))
        src = part.at[j, pl.ds(k * CW, CW)] if s == 0 else rl.at[k, s - 1]
        return rcopy(src, rl.at[k, s], l_s.at[k, s], l_r.at[k, s], (y_dn, fs))

    def short_copy(k, s):
        j = at_y(y + sgn * (SHORT - s))
        src = part.at[j, pl.ds(k * CW, CW)] if s == 0 else rs.at[k, s - 1]
        return rcopy(src, rs.at[k, s], s_s.at[k, s], s_r.at[k, s], (y_up, fs))

    def product(k):
        for d in range(1, NF):
            frm = fdev(NF - d)
            rcopy(parts.at[k, frm], parts.at[k, frm], pk_s.at[k, d - 1], pk_r.at[k, d - 1], (dp, frm)).wait_recv()
        a = parts[k].reshape(NF * SLOTS, CW)
        b = cots[...].reshape(NF * SLOTS, KV)
        p = dot(a, b, 0, 0)
        for j in range(NY):
            part[j, k * CW:(k + 1) * CW] = p[:, j * LANE:(j + 1) * LANE]
        go(long_copy(k, 0))
        go(short_copy(k, 0))

    def ring_step(k, s):
        here = pl.ds(k * CW, CW)
        long_copy(k, s - 1).wait_recv()
        if s < LONG:
            rl[k, s - 1] += part[at_y(y - sgn * (LONG - s)), here]
            go(long_copy(k, s))
        if s <= SHORT:
            short_copy(k, s - 1).wait_recv()
        if s < SHORT:
            rs[k, s - 1] += part[at_y(y + sgn * (SHORT - s)), here]
            go(short_copy(k, s))
        if s == LONG:
            red[here] = part[y, here] + rl[k, LONG - 1] + rs[k, SHORT - 1]

    red[W:] = jnp.zeros((NZ * ZR - W, LANE), f32)

    def slot_grads():
        for g in range(2):
            b = cots[g * 4:(g + 1) * 4].reshape(4 * SLOTS, KV)
            q = dot(b, wt[...], 1, 1).astype(bf16)
            slot[g * 4:(g + 1) * 4] = q.reshape(4, SLOTS, W)
        for d in (2, 6, 3, 7, 4, 5, 1):
            to = fdev(d)
            go(rcopy(slot.at[to], own.at[fs], sg_s.at[d - 1], sg_r.at[d - 1], (dp, to)))
        own[fs] = slot[fs]

    product(0)
    slot_grads()
    for t in range(1, CH + LONG):
        if t < CH:
            product(t)
        for s in range(min(t, LONG), 0, -1):
            k = t - s
            if k < CH:
                ring_step(k, s)

    for d in (6, 5, 7, 4, 8, 3, 9, 2, 10, 1, 11):
        to = zdev(d)
        src = red.at[pl.ds(pl.multiple_of(to * ZR, 16), ZR)]
        go(rcopy(src, zrecv.at[d - 1], z_s.at[d - 1], z_r.at[d - 1], (y * NZ + to, fs)))

    for d in range(1, NF):
        frm = fdev(NF - d)
        rcopy(own.at[frm], own.at[frm], sg_s.at[d - 1], sg_r.at[d - 1], (dp, frm)).wait_recv()
    hot_s = hot[:, :SLOTS]
    for f in range(NF):
        gt[:, f * W:(f + 1) * W] = dot(hot_s, own[f], 1, 0).astype(bf16)
    gt_copy = pltpu.make_async_copy(gt, gt_out, out_s.at[NY])
    gt_copy.start()

    total = red[pl.ds(pl.multiple_of(z * ZR, 16), ZR)]
    for d in range(1, NZ):
        rcopy(zrecv.at[d - 1], zrecv.at[d - 1], z_s.at[d - 1], z_r.at[d - 1], (dp, fs)).wait_recv()
        total += zrecv[d - 1]
    zsum[...] = total / scale[0]

    mine = full.at[y, pl.ds(pl.multiple_of(z * ZR, 16), ZR)]
    for d in (6, 5, 7, 4, 8, 3, 9, 2, 10, 1, 11):
        go(rcopy(zsum, mine, az_s.at[d - 1], az_r.at[d - 1], (y * NZ + zdev(d), fs)))
    mine[...] = zsum[...]
    for d in range(1, NZ):
        there = full.at[y, pl.ds(pl.multiple_of(zdev(NZ - d) * ZR, 16), ZR)]
        rcopy(zsum, there, az_s.at[d - 1], az_r.at[d - 1], (dp, fs)).wait_recv()

    outs = []

    def put(j, i):
        cp = pltpu.make_async_copy(
            full.at[j, pl.ds(0, W)],
            gw_out.at[:, pl.ds(pl.multiple_of(j * LANE, LANE), LANE)], out_s.at[i]
        )
        cp.start()
        outs.append(cp)

    half = W // 2

    def along(s, h, up):
        j = at_y(y - sgn * s) if up else at_y(y + sgn * s)
        ref = full.at[j, pl.ds(h * half, half)]
        if up:
            return rcopy(ref, ref, al_s.at[s, h], al_r.at[s, h], (y_up, fs))
        return rcopy(ref, ref, as_s.at[s, h], as_r.at[s, h], (y_dn, fs))

    def arrived(s, h, up):
        j = at_y(y - sgn * (s + 1)) if up else at_y(y + sgn * (s + 1))
        ref = full.at[j, pl.ds(h * half, half)]
        sems = (al_s.at[s, h], al_r.at[s, h]) if up else (as_s.at[s, h], as_r.at[s, h])
        rcopy(ref, ref, *sems, (dp, fs)).wait_recv()
        return j

    for h in range(2):
        go(along(0, h, True))
        go(along(0, h, False))
    put(y, 0)
    for s in range(1, LONG + 1):
        for h in range(2):
            j = arrived(s - 1, h, True)
            if s < LONG:
                go(along(s, h, True))
            if s <= SHORT:
                i = arrived(s - 1, h, False)
                if s < SHORT:
                    go(along(s, h, False))
        put(j, s)
        if s <= SHORT:
            put(i, LONG + s)

    for cp in sends:
        cp.wait_send()
    for cp in outs:
        cp.wait()
    gt_copy.wait()


def shards(tokens, value_grad, value_weight, counts, chosen_rows, loss_scale):
    n = chosen_rows.shape[1]
    live = lax.broadcasted_iota(jnp.int32, (1, n), 1) < counts[0]
    sel = jnp.pad(jnp.where(live, chosen_rows, -1), ((0, 7), (0, ROWS - n)), constant_values=-1)
    vmem = pl.BlockSpec(memory_space=pltpu.VMEM)
    dma = pltpu.SemaphoreType.DMA
    scratch = [
        pltpu.VMEM((SLOTS, D), bf16),
        pltpu.VMEM((NF, SLOTS, KV), bf16),
        pltpu.VMEM((CH, NF, SLOTS, CW), bf16),
        pltpu.VMEM((NF, SLOTS, W), bf16),
        pltpu.VMEM((NF, SLOTS, W), bf16),
        pltpu.VMEM((ROWS, D), bf16),
        pltpu.VMEM((NY, W, LANE), f32),
        pltpu.VMEM((CH, LONG, CW, LANE), f32),
        pltpu.VMEM((CH, SHORT, CW, LANE), f32),
        pltpu.VMEM((NZ * ZR, LANE), f32),
        pltpu.VMEM((NZ - 1, ZR, LANE), f32),
        pltpu.VMEM((ZR, LANE), f32),
        pltpu.VMEM((NY, NZ * ZR, LANE), f32),
        dma((3,)), dma((3,)), dma((4,)), dma((4,)),
        dma((CH, NF - 1)), dma((CH, NF - 1)), dma((NF - 1,)), dma((NF - 1,)),
        dma((CH, LONG)), dma((CH, LONG)), dma((CH, SHORT)), dma((CH, SHORT)),
        dma((NZ - 1,)), dma((NZ - 1,)), dma((NZ - 1,)), dma((NZ - 1,)),
        dma((LONG, 2)), dma((LONG, 2)), dma((SHORT, 2)), dma((SHORT, 2)),
        dma((NY + 1,)),
    ]
    return pl.pallas_call(
        kernel,
        out_shape=(
            jax.ShapeDtypeStruct((ROWS, D), bf16),
            jax.ShapeDtypeStruct((W, KV), f32),
        ),
        in_specs=[vmem] * 4 + [pl.BlockSpec(memory_space=pltpu.SMEM)],
        out_specs=(pl.BlockSpec(memory_space=pl.ANY), pl.BlockSpec(memory_space=pl.ANY)),
        scratch_shapes=scratch,
        compiler_params=pltpu.CompilerParams(
            collective_id=0, has_side_effects=True, vmem_limit_bytes=48 << 20
        ),
    )(tokens, value_grad, value_weight, sel, loss_scale)


def solution(mesh):
    return jax.shard_map(
        shards,
        mesh=mesh,
        in_specs=(
            P(("dp", "fsdp"), None),
            P(("dp", "fsdp"), None),
            P("fsdp", None),
            P(("dp", "fsdp")),
            P(("dp", "fsdp"), None),
            P(),
        ),
        out_specs=(P(("dp", "fsdp"), None), P("fsdp", None)),
        check_vma=False,
    )
```

```python
import jax
import jax.numpy as jnp
from jax import lax
from jax.experimental import pallas as pl
from jax.experimental.pallas import tpu as pltpu
from jax.sharding import PartitionSpec as P

MESH = pl.DeviceIdType.MESH
NY, NZ, NF = 8, 12, 8
SLOTS = 96
ROWS, D, KV = 128, 4096, 1024
W = D // NF
CH = 4
CW = W // CH
ZR = 48
LANE = KV // NY
LONG, SHORT = NY // 2, NY // 2 - 1
f32, bf16 = jnp.float32, jnp.bfloat16
TOP, LOW = 2.0 ** 15.4, 2.0 ** -15.4


def dot(a, b, ca, cb):
    return lax.dot_general(a, b, (((ca,), (cb,)), ((), ())), preferred_element_type=f32)


def kernel(
    tok_in, vg_in, wt_in, count, chosen, scale, gt_out, gw_out,
    tok, vg, wt, sel, picked, cots, parts, slot, own, part, el, es, rl, rs, red, ered, zrecv, zsum, full, xb, yb, zb,
    gt, gw, in_s, out_s, xb_s, xb_r, yb_s, yb_r, zb_s, zb_r, cot_s, cot_r, sib_s, sib_r, pk_s, pk_r, sg_s, sg_r,
    l_s, l_r, s_s, s_r, z_s, z_r, az_s, az_r, al_s, al_r, as_s, as_r,
):
    dp, fs = lax.axis_index("dp"), lax.axis_index("fsdp")
    y, z = dp // NZ, lax.rem(dp, NZ)
    c, x = lax.rem(fs, 2), fs // 2
    sgn = 1 - 2 * c
    sib = x * 2 + 1 - c

    def at_y(v):
        return lax.rem(v + 2 * NY, NY)

    ins = [pltpu.make_async_copy(a, b, in_s.at[i]) for i, (a, b) in enumerate(((vg_in, vg), (tok_in, tok), (wt_in, wt)))]
    for cp in ins:
        cp.start()

    y_up, y_dn = at_y(y + sgn) * NZ + z, at_y(y - sgn) * NZ + z

    def zdev(d):
        return lax.rem(z + d, NZ)

    def ydev(d):
        return at_y(y + d) * NZ + z

    def fdev(d):
        return lax.rem(fs + d, NF)

    def xdev(d):
        return lax.rem(x + d, 4) * 2 + c

    def rcopy(src, dst, ss, rs_, dev):
        return pltpu.make_async_remote_copy(
            src_ref=src, dst_ref=dst, send_sem=ss, recv_sem=rs_, device_id=dev, device_id_type=MESH
        )

    barrier = pltpu.get_barrier_semaphore()
    peers = [(dp, fdev(d)) for d in range(1, NF)]
    peers += [(ydev(d), fs) for d in range(1, NY)]
    peers += [(y * NZ + zdev(d), fs) for d in range(1, NZ)]
    for peer in peers:
        pl.semaphore_signal(barrier, inc=1, device_id=peer, device_id_type=MESH)

    n = chosen.shape[1]
    sel[...] = jnp.full(sel.shape, -1, jnp.int32)
    live = lax.broadcasted_iota(jnp.int32, (1, n), 1) < count[0]
    sel[0:1, 0:n] = jnp.where(live, chosen[...], -1)
    rows = lax.broadcasted_iota(jnp.int32, (ROWS, ROWS), 0)
    hot = jnp.where(rows == sel[0:1, :], 1.0, 0.0).astype(bf16)

    def widest(v):
        t = jnp.sum(v * v, axis=0, keepdims=True)
        return jnp.max(t, axis=1, keepdims=True)

    ins[0].wait()
    v = dot(hot, vg[...], 0, 0)[:SLOTS]
    cots[fs] = v.astype(bf16)
    g_sq = widest(v)
    ins[1].wait()
    t_sq = jnp.zeros((1, 1), f32)
    for b in range(4):
        cols = slice(b * 1024, (b + 1) * 1024)
        v = dot(hot, tok[:, cols], 0, 0)[:SLOTS]
        picked[:, cols] = v.astype(bf16)
        t_sq = jnp.maximum(t_sq, widest(v))
    xb[0] = jnp.broadcast_to(jnp.sqrt(t_sq) * jnp.sqrt(g_sq), xb.shape[1:])
    pl.semaphore_wait(barrier, len(peers))

    sends = []

    def go(cp):
        cp.start()
        sends.append(cp)

    def bounds(buf, ss, rs_, devs):
        for d, dev in enumerate(devs):
            go(rcopy(buf.at[0], buf.at[d + 1], ss.at[d], rs_.at[d], dev))

    def largest(buf, ss, rs_):
        top = buf[0]
        for d in range(buf.shape[0] - 1):
            rcopy(buf.at[d + 1], buf.at[d + 1], ss.at[d], rs_.at[d], (dp, fs)).wait_recv()
            top = jnp.maximum(top, buf[d + 1])
        return top

    bounds(xb, xb_s, xb_r, [(dp, fdev(d)) for d in range(1, NF)])

    for d in (1, 3, 2):
        go(rcopy(cots.at[fs], cots.at[fs], cot_s.at[d - 1], cot_r.at[d - 1], (dp, xdev(d))))
    go(rcopy(cots.at[fs], cots.at[fs], sib_s.at[0], sib_r.at[0], (dp, sib)))

    for k in range(CH):
        for d in (2, 6, 3, 7, 4, 5, 1):
            to = fdev(d)
            cols = pl.ds(pl.multiple_of(to * W + k * CW, CW), CW)
            go(rcopy(picked.at[:, cols], parts.at[k, fs], pk_s.at[k, d - 1], pk_r.at[k, d - 1], (dp, to)))
        cols = pl.ds(pl.multiple_of(fs * W + k * CW, CW), CW)
        parts[k, fs] = picked[:, cols]

    yb[0] = largest(xb, xb_s, xb_r)
    bounds(yb, yb_s, yb_r, [(ydev(d), fs) for d in range(1, NY)])

    for d in (1, 3, 2):
        frm = xdev(4 - d)
        rcopy(cots.at[frm], cots.at[frm], cot_s.at[d - 1], cot_r.at[d - 1], (dp, frm)).wait_recv()
        go(rcopy(cots.at[frm], cots.at[frm], sib_s.at[d], sib_r.at[d], (dp, sib)))
    for d in range(4):
        frm = lax.rem(x + 4 - d, 4) * 2 + 1 - c
        rcopy(cots.at[frm], cots.at[frm], sib_s.at[d], sib_r.at[d], (dp, sib)).wait_recv()

    def steps(bound):
        a = TOP / jnp.maximum(bound[0:1], 1e-30)
        return a, 1.0 / a

    def code(v, a):
        w = LOW + a * jnp.abs(v)
        w = w * w
        w = w * w
        w = w * w
        return jnp.where(v < 0, -w, w).astype(bf16)

    def value(e, i):
        e = e.astype(f32)
        r = lax.rsqrt(lax.rsqrt(jnp.abs(e)))
        w = (r * lax.rsqrt(r) - LOW) * i
        return jnp.where(e < 0, -w, w)

    zb[0] = largest(yb, yb_s, yb_r)
    bounds(zb, zb_s, zb_r, [(y * NZ + zdev(d), fs) for d in range(1, NZ)])
    y_a, y_i = steps(zb[0] * (NF * NY))
    z_a = z_i = None

    def long_copy(k, s):
        src = el.at[k, s]
        return rcopy(src, rl.at[k, s], l_s.at[k, s], l_r.at[k, s], (y_dn, fs))

    def short_copy(k, s):
        src = es.at[k, s]
        return rcopy(src, rs.at[k, s], s_s.at[k, s], s_r.at[k, s], (y_up, fs))

    def product(k):
        for d in range(1, NF):
            frm = fdev(NF - d)
            rcopy(parts.at[k, frm], parts.at[k, frm], pk_s.at[k, d - 1], pk_r.at[k, d - 1], (dp, frm)).wait_recv()
        a = parts[k].reshape(NF * SLOTS, CW)
        b = cots[...].reshape(NF * SLOTS, KV)
        p = dot(a, b, 0, 0)
        for j in range(NY):
            part[j, k * CW:(k + 1) * CW] = p[:, j * LANE:(j + 1) * LANE]
        here = pl.ds(k * CW, CW)
        el[k, 0] = code(part[at_y(y - sgn * LONG), here], y_a)
        go(long_copy(k, 0))
        es[k, 0] = code(part[at_y(y + sgn * SHORT), here], y_a)
        go(short_copy(k, 0))

    def ring_step(k, s):
        here = pl.ds(k * CW, CW)
        long_copy(k, s - 1).wait_recv()
        if s < LONG:
            el[k, s] = code(part[at_y(y - sgn * (LONG - s)), here] + value(rl[k, s - 1], y_i), y_a)
            go(long_copy(k, s))
        if s <= SHORT:
            short_copy(k, s - 1).wait_recv()
        if s < SHORT:
            es[k, s] = code(part[at_y(y + sgn * (SHORT - s)), here] + value(rs[k, s - 1], y_i), y_a)
            go(short_copy(k, s))
        if s == LONG:
            total = part[y, here] + value(rl[k, LONG - 1], y_i) + value(rs[k, SHORT - 1], y_i)
            red[here] = total
            ered[here] = code(total, z_a)

    red[W:] = jnp.zeros((NZ * ZR - W, LANE), f32)
    ered[W:] = jnp.zeros((NZ * ZR - W, LANE), bf16)

    def slot_grads():
        for g in range(2):
            b = cots[g * 4:(g + 1) * 4].reshape(4 * SLOTS, KV)
            q = dot(b, wt[...], 1, 1).astype(bf16)
            slot[g * 4:(g + 1) * 4] = q.reshape(4, SLOTS, W)
        for d in (2, 6, 3, 7, 4, 5, 1):
            to = fdev(d)
            go(rcopy(slot.at[to], own.at[fs], sg_s.at[d - 1], sg_r.at[d - 1], (dp, to)))
        own[fs] = slot[fs]

    product(0)
    ins[2].wait()
    slot_grads()
    z_a, z_i = steps(largest(zb, zb_s, zb_r) * (NF * NY * NZ))
    for t in range(1, CH + LONG):
        if t < CH:
            product(t)
        for s in range(min(t, LONG), 0, -1):
            k = t - s
            if k < CH:
                ring_step(k, s)

    for d in (6, 5, 7, 4, 8, 3, 9, 2, 10, 1, 11):
        to = zdev(d)
        src = ered.at[pl.ds(pl.multiple_of(to * ZR, 16), ZR)]
        go(rcopy(src, zrecv.at[d - 1], z_s.at[d - 1], z_r.at[d - 1], (y * NZ + to, fs)))

    for d in range(1, NF):
        frm = fdev(NF - d)
        rcopy(own.at[frm], own.at[frm], sg_s.at[d - 1], sg_r.at[d - 1], (dp, frm)).wait_recv()
    hot_s = hot[:, :SLOTS]
    for f in range(NF):
        gt[:, f * W:(f + 1) * W] = dot(hot_s, own[f], 1, 0).astype(bf16)

    outs = [pltpu.make_async_copy(gt, gt_out, out_s.at[NY])]
    outs[0].start()
    total = red[pl.ds(pl.multiple_of(z * ZR, 16), ZR)]
    for d in range(1, NZ):
        rcopy(zrecv.at[d - 1], zrecv.at[d - 1], z_s.at[d - 1], z_r.at[d - 1], (dp, fs)).wait_recv()
        total += value(zrecv[d - 1], z_i)
    zsum[...] = code(total, z_a)

    mine = full.at[y, pl.ds(pl.multiple_of(z * ZR, 16), ZR)]
    for d in (6, 5, 7, 4, 8, 3, 9, 2, 10, 1, 11):
        go(rcopy(zsum, mine, az_s.at[d - 1], az_r.at[d - 1], (y * NZ + zdev(d), fs)))
    mine[...] = zsum[...]
    for d in range(1, NZ):
        there = full.at[y, pl.ds(pl.multiple_of(zdev(NZ - d) * ZR, 16), ZR)]
        rcopy(zsum, there, az_s.at[d - 1], az_r.at[d - 1], (dp, fs)).wait_recv()

    out_i = z_i / scale[0]

    def put(j):
        i = len(outs) - 1
        gw[i] = value(full[j, 0:W], out_i)
        cp = pltpu.make_async_copy(gw.at[i], gw_out.at[:, pl.ds(pl.multiple_of(j * LANE, LANE), LANE)], out_s.at[i])
        cp.start()
        outs.append(cp)

    half = W // 2

    def along(s, h, up):
        j = at_y(y - sgn * s) if up else at_y(y + sgn * s)
        ref = full.at[j, pl.ds(h * half, half)]
        if up:
            return rcopy(ref, ref, al_s.at[s, h], al_r.at[s, h], (y_up, fs))
        return rcopy(ref, ref, as_s.at[s, h], as_r.at[s, h], (y_dn, fs))

    def arrived(s, h, up):
        j = at_y(y - sgn * (s + 1)) if up else at_y(y + sgn * (s + 1))
        ref = full.at[j, pl.ds(h * half, half)]
        sems = (al_s.at[s, h], al_r.at[s, h]) if up else (as_s.at[s, h], as_r.at[s, h])
        rcopy(ref, ref, *sems, (dp, fs)).wait_recv()
        return j

    for h in range(2):
        go(along(0, h, True))
        go(along(0, h, False))
    put(y)
    for s in range(1, LONG + 1):
        for h in range(2):
            j = arrived(s - 1, h, True)
            if s < LONG:
                go(along(s, h, True))
            if s <= SHORT:
                i = arrived(s - 1, h, False)
                if s < SHORT:
                    go(along(s, h, False))
        put(j)
        if s <= SHORT:
            put(i)

    for cp in sends:
        cp.wait_send()
    for cp in outs:
        cp.wait()


def shards(tokens, value_grad, value_weight, counts, chosen_rows, loss_scale):
    vmem = pl.BlockSpec(memory_space=pltpu.VMEM)
    hbm, smem = pl.BlockSpec(memory_space=pltpu.HBM), pl.BlockSpec(memory_space=pltpu.SMEM)
    dma = pltpu.SemaphoreType.DMA
    scratch = [
        pltpu.VMEM((ROWS, D), bf16),
        pltpu.VMEM((ROWS, KV), bf16),
        pltpu.VMEM((W, KV), bf16),
        pltpu.VMEM((8, ROWS), jnp.int32),
        pltpu.VMEM((SLOTS, D), bf16),
        pltpu.VMEM((NF, SLOTS, KV), bf16),
        pltpu.VMEM((CH, NF, SLOTS, CW), bf16),
        pltpu.VMEM((NF, SLOTS, W), bf16),
        pltpu.VMEM((NF, SLOTS, W), bf16),
        pltpu.VMEM((NY, W, LANE), f32),
        pltpu.VMEM((CH, LONG, CW, LANE), bf16),
        pltpu.VMEM((CH, SHORT, CW, LANE), bf16),
        pltpu.VMEM((CH, LONG, CW, LANE), bf16),
        pltpu.VMEM((CH, SHORT, CW, LANE), bf16),
        pltpu.VMEM((NZ * ZR, LANE), f32),
        pltpu.VMEM((NZ * ZR, LANE), bf16),
        pltpu.VMEM((NZ - 1, ZR, LANE), bf16),
        pltpu.VMEM((ZR, LANE), bf16),
        pltpu.VMEM((NY, NZ * ZR, LANE), bf16),
        pltpu.VMEM((NF, 8, LANE), f32),
        pltpu.VMEM((NY, 8, LANE), f32),
        pltpu.VMEM((NZ, 8, LANE), f32),
        pltpu.VMEM((ROWS, D), bf16),
        pltpu.VMEM((NY, W, LANE), f32),
        dma((3,)), dma((NY + 1,)), dma((NF - 1,)), dma((NF - 1,)), dma((NY - 1,)), dma((NY - 1,)), dma((NZ - 1,)), dma((NZ - 1,)),
        dma((3,)), dma((3,)), dma((4,)), dma((4,)),
        dma((CH, NF - 1)), dma((CH, NF - 1)), dma((NF - 1,)), dma((NF - 1,)),
        dma((CH, LONG)), dma((CH, LONG)), dma((CH, SHORT)), dma((CH, SHORT)),
        dma((NZ - 1,)), dma((NZ - 1,)), dma((NZ - 1,)), dma((NZ - 1,)),
        dma((LONG, 2)), dma((LONG, 2)), dma((SHORT, 2)), dma((SHORT, 2)),
    ]
    return pl.pallas_call(
        kernel,
        out_shape=(
            jax.ShapeDtypeStruct((ROWS, D), bf16),
            jax.ShapeDtypeStruct((W, KV), f32),
        ),
        in_specs=[hbm] * 3 + [smem, vmem, smem],
        out_specs=(hbm, hbm),
        scratch_shapes=scratch,
        compiler_params=pltpu.CompilerParams(
            collective_id=0, has_side_effects=True, vmem_limit_bytes=60 << 20
        ),
    )(tokens, value_grad, value_weight, counts, chosen_rows, loss_scale)


def solution(mesh):
    return jax.shard_map(
        shards,
        mesh=mesh,
        in_specs=(
            P(("dp", "fsdp"), None),
            P(("dp", "fsdp"), None),
            P("fsdp", None),
            P(("dp", "fsdp")),
            P(("dp", "fsdp"), None),
            P(),
        ),
        out_specs=(P(("dp", "fsdp"), None), P("fsdp", None)),
        check_vma=False,
    )
```

```python
import jax
import jax.numpy as jnp
from jax import lax
from jax.experimental import pallas as pl
from jax.experimental.pallas import tpu as pltpu
from jax.sharding import PartitionSpec as P

MESH = pl.DeviceIdType.MESH
NY, NZ, NF = 8, 12, 8
SLOTS = 96
ROWS, D, KV = 128, 4096, 1024
W = D // NF
CH = 4
CW = W // CH
ZR = 48
LANE = KV // NY
LONG, SHORT = NY // 2, NY // 2 - 1
f32, bf16 = jnp.float32, jnp.bfloat16
TOP, LOW = 2.0 ** 15.4, 2.0 ** -15.4


def dot(a, b, ca, cb):
    return lax.dot_general(a, b, (((ca,), (cb,)), ((), ())), preferred_element_type=f32)


def kernel(
    tok_in, vg_in, wt_in, count, chosen, scale, gt_out, gw_out,
    tok, vg, wt, sel, picked, cots, parts, slot, own, part, el, es, rl, rs, red, ered, zrecv, zsum, full, xb, yb, zb,
    gt, gw, in_s, out_s, xb_s, xb_r, yb_s, yb_r, zb_s, zb_r, cot_s, cot_r, sib_s, sib_r, pk_s, pk_r, sg_s, sg_r,
    l_s, l_r, s_s, s_r, z_s, z_r, az_s, az_r, al_s, al_r, as_s, as_r,
):
    dp, fs = lax.axis_index("dp"), lax.axis_index("fsdp")
    y, z = dp // NZ, lax.rem(dp, NZ)
    c, x = lax.rem(fs, 2), fs // 2
    sgn = 1 - 2 * c
    sib = x * 2 + 1 - c

    def at_y(v):
        return lax.rem(v + 2 * NY, NY)

    ins = [pltpu.make_async_copy(a, b, in_s.at[i]) for i, (a, b) in enumerate(((vg_in, vg), (tok_in, tok), (wt_in, wt)))]
    for cp in ins:
        cp.start()

    y_up, y_dn = at_y(y + sgn) * NZ + z, at_y(y - sgn) * NZ + z

    def zdev(d):
        return lax.rem(z + d, NZ)

    def ydev(d):
        return at_y(y + d) * NZ + z

    def fdev(d):
        return lax.rem(fs + d, NF)

    def xdev(d):
        return lax.rem(x + d, 4) * 2 + c

    def rcopy(src, dst, ss, rs_, dev):
        return pltpu.make_async_remote_copy(
            src_ref=src, dst_ref=dst, send_sem=ss, recv_sem=rs_, device_id=dev, device_id_type=MESH
        )

    barrier = pltpu.get_barrier_semaphore()
    peers = [(dp, fdev(d)) for d in range(1, NF)]
    peers += [(ydev(d), fs) for d in range(1, NY)]
    peers += [(y * NZ + zdev(d), fs) for d in range(1, NZ)]
    for peer in peers:
        pl.semaphore_signal(barrier, inc=1, device_id=peer, device_id_type=MESH)

    n = chosen.shape[1]
    sel[...] = jnp.full(sel.shape, -1, jnp.int32)
    live = lax.broadcasted_iota(jnp.int32, (1, n), 1) < count[0]
    sel[0:1, 0:n] = jnp.where(live, chosen[...], -1)
    rows = lax.broadcasted_iota(jnp.int32, (ROWS, ROWS), 0)
    hot = jnp.where(rows == sel[0:1, :], 1.0, 0.0).astype(bf16)

    def widest(v):
        t = jnp.sum(v * v, axis=0, keepdims=True)
        return jnp.max(t, axis=1, keepdims=True)

    ins[0].wait()
    v = dot(hot, vg[...], 0, 0)[:SLOTS]
    cots[fs] = v.astype(bf16)
    g_sq = widest(v)
    ins[1].wait()
    t_sq = jnp.zeros((1, 1), f32)
    for b in range(4):
        cols = slice(b * 1024, (b + 1) * 1024)
        v = dot(hot, tok[:, cols], 0, 0)[:SLOTS]
        picked[:, cols] = v.astype(bf16)
        t_sq = jnp.maximum(t_sq, widest(v))
    xb[0] = jnp.broadcast_to(jnp.sqrt(t_sq) * jnp.sqrt(g_sq), xb.shape[1:])
    pl.semaphore_wait(barrier, len(peers))

    sends = []

    def go(cp):
        cp.start()
        sends.append(cp)

    def bounds(buf, ss, rs_, devs):
        for d, dev in enumerate(devs):
            go(rcopy(buf.at[0], buf.at[d + 1], ss.at[d], rs_.at[d], dev))

    def largest(buf, ss, rs_):
        top = buf[0]
        for d in range(buf.shape[0] - 1):
            rcopy(buf.at[d + 1], buf.at[d + 1], ss.at[d], rs_.at[d], (dp, fs)).wait_recv()
            top = jnp.maximum(top, buf[d + 1])
        return top

    bounds(xb, xb_s, xb_r, [(dp, fdev(d)) for d in range(1, NF)])

    fwd, back = xdev(sgn + 4), xdev(4 - sgn)
    across = xdev(2)
    mine = cots.at[fs]
    go(rcopy(mine, mine, cot_s.at[0], cot_r.at[0], (dp, fwd)))
    go(rcopy(mine, mine, cot_s.at[1], cot_r.at[1], (dp, back)))
    go(rcopy(mine, mine, sib_s.at[0], sib_r.at[0], (dp, sib)))

    def cot_in(i, frm):
        ref = cots.at[frm]
        rcopy(ref, ref, cot_s.at[i], cot_r.at[i], (dp, frm)).wait_recv()
        if i == 0:
            go(rcopy(ref, ref, cot_s.at[2], cot_r.at[2], (dp, fwd)))
        go(rcopy(ref, ref, sib_s.at[i + 1], sib_r.at[i + 1], (dp, sib)))

    for k in range(CH):
        for d in (2, 6, 3, 7, 4, 5, 1):
            to = fdev(d)
            cols = pl.ds(pl.multiple_of(to * W + k * CW, CW), CW)
            go(rcopy(picked.at[:, cols], parts.at[k, fs], pk_s.at[k, d - 1], pk_r.at[k, d - 1], (dp, to)))
        cols = pl.ds(pl.multiple_of(fs * W + k * CW, CW), CW)
        parts[k, fs] = picked[:, cols]
        if k == 0:
            cot_in(0, back)

    yb[0] = largest(xb, xb_s, xb_r)
    bounds(yb, yb_s, yb_r, [(ydev(d), fs) for d in range(1, NY)])

    cot_in(1, fwd)
    cot_in(2, across)
    for i, v in enumerate((0, sgn, -sgn, 2)):
        ref = cots.at[lax.rem(x + v + 4, 4) * 2 + 1 - c]
        rcopy(ref, ref, sib_s.at[i], sib_r.at[i], (dp, sib)).wait_recv()

    def steps(bound):
        a = TOP / jnp.maximum(bound[0:1], 1e-30)
        return a, 1.0 / a

    def code(v, a):
        w = LOW + a * jnp.abs(v)
        w = w * w
        w = w * w
        w = w * w
        return jnp.where(v < 0, -w, w).astype(bf16)

    def value(e, i):
        e = e.astype(f32)
        r = lax.rsqrt(lax.rsqrt(jnp.abs(e)))
        w = (r * lax.rsqrt(r) - LOW) * i
        return jnp.where(e < 0, -w, w)

    zb[0] = largest(yb, yb_s, yb_r)
    bounds(zb, zb_s, zb_r, [(y * NZ + zdev(d), fs) for d in range(1, NZ)])
    y_a, y_i = steps(zb[0] * (NF * NY))
    z_a = z_i = None

    def long_copy(k, s):
        src = el.at[k, s]
        return rcopy(src, rl.at[k, s], l_s.at[k, s], l_r.at[k, s], (y_dn, fs))

    def short_copy(k, s):
        src = es.at[k, s]
        return rcopy(src, rs.at[k, s], s_s.at[k, s], s_r.at[k, s], (y_up, fs))

    def product(k):
        for d in range(1, NF):
            frm = fdev(NF - d)
            rcopy(parts.at[k, frm], parts.at[k, frm], pk_s.at[k, d - 1], pk_r.at[k, d - 1], (dp, frm)).wait_recv()
        a = parts[k].reshape(NF * SLOTS, CW)
        b = cots[...].reshape(NF * SLOTS, KV)
        p = dot(a, b, 0, 0)
        for j in range(NY):
            part[j, k * CW:(k + 1) * CW] = p[:, j * LANE:(j + 1) * LANE]
        here = pl.ds(k * CW, CW)
        el[k, 0] = code(part[at_y(y - sgn * LONG), here], y_a)
        go(long_copy(k, 0))
        es[k, 0] = code(part[at_y(y + sgn * SHORT), here], y_a)
        go(short_copy(k, 0))

    def ring_step(k, s):
        here = pl.ds(k * CW, CW)
        long_copy(k, s - 1).wait_recv()
        if s < LONG:
            el[k, s] = code(part[at_y(y - sgn * (LONG - s)), here] + value(rl[k, s - 1], y_i), y_a)
            go(long_copy(k, s))
        if s <= SHORT:
            short_copy(k, s - 1).wait_recv()
        if s < SHORT:
            es[k, s] = code(part[at_y(y + sgn * (SHORT - s)), here] + value(rs[k, s - 1], y_i), y_a)
            go(short_copy(k, s))
        if s == LONG:
            total = part[y, here] + value(rl[k, LONG - 1], y_i) + value(rs[k, SHORT - 1], y_i)
            red[k, 0:CW] = total
            ered[k, 0:CW] = code(total, z_a)
            for r in range(3):
                to = 3 * k + r
                d = lax.rem(to - z + NZ, NZ)

                @pl.when(to != z)
                def _():
                    src = ered.at[k, pl.ds(r * ZR, ZR)]
                    rcopy(src, zrecv.at[d - 1], z_s.at[d - 1], z_r.at[d - 1], (y * NZ + to, fs)).start()

    red[:, CW:] = jnp.zeros((CH, 3 * ZR - CW, LANE), f32)
    ered[:, CW:] = jnp.ones((CH, 3 * ZR - CW, LANE), bf16)

    def slot_grads():
        for g in range(2):
            b = cots[g * 4:(g + 1) * 4].reshape(4 * SLOTS, KV)
            q = dot(b, wt[...], 1, 1).astype(bf16)
            slot[g * 4:(g + 1) * 4] = q.reshape(4, SLOTS, W)
        for d in (2, 6, 3, 7, 4, 5, 1):
            to = fdev(d)
            go(rcopy(slot.at[to], own.at[fs], sg_s.at[d - 1], sg_r.at[d - 1], (dp, to)))
        own[fs] = slot[fs]

    def z_sum(k):
        @pl.when(z // 3 == k)
        def _():
            part_z = pl.ds(pl.multiple_of(lax.rem(z, 3) * ZR, 16), ZR)
            total = red[k, part_z]
            for d in (1, 11, 2, 10, 3, 9, 4, 8, 5, 7, 6):
                rcopy(zrecv.at[d - 1], zrecv.at[d - 1], z_s.at[d - 1], z_r.at[d - 1], (dp, fs)).wait_recv()
                total += value(zrecv[d - 1], z_i)
            zsum[...] = code(total, z_a)
            for d in (6, 5, 7, 4, 8, 3, 9, 2, 10, 1, 11):
                rcopy(zsum, full.at[y, k, part_z], az_s.at[d - 1], az_r.at[d - 1], (y * NZ + zdev(d), fs)).start()
            full[y, k, part_z] = zsum[...]

    def along(k, s, up):
        ref = full.at[at_y(y - sgn * s) if up else at_y(y + sgn * s), k, pl.ds(0, CW)]
        if up:
            return rcopy(ref, ref, al_s.at[k, s], al_r.at[k, s], (y_up, fs))
        return rcopy(ref, ref, as_s.at[k, s], as_r.at[k, s], (y_dn, fs))

    def arrived(k, s, up):
        j = at_y(y - sgn * (s + 1)) if up else at_y(y + sgn * (s + 1))
        ref = full.at[j, k, pl.ds(0, CW)]
        sems = (al_s.at[k, s], al_r.at[k, s]) if up else (as_s.at[k, s], as_r.at[k, s])
        rcopy(ref, ref, *sems, (dp, fs)).wait_recv()
        return j

    def put(k, j):
        gw[k * CW:(k + 1) * CW, pl.ds(pl.multiple_of(j * LANE, LANE), LANE)] = value(full[j, k, 0:CW], z_i / scale[0])

    def z_in(k):
        for r in range(3):
            frm = 3 * k + r
            d = lax.rem(z - frm + NZ, NZ)

            @pl.when(frm != z)
            def _():
                ref = full.at[y, k, pl.ds(r * ZR, ZR)]
                rcopy(ref, ref, az_s.at[d - 1], az_r.at[d - 1], (dp, fs)).wait_recv()
        go(along(k, 0, True))
        go(along(k, 0, False))
        put(k, y)

    outs = []

    def out(src, dst, i):
        cp = pltpu.make_async_copy(src, dst, out_s.at[i])
        cp.start()
        outs.append(cp)

    def y_step(k, s):
        js = [arrived(k, s - 1, True)]
        if s < LONG:
            go(along(k, s, True))
        if s <= SHORT:
            js.append(arrived(k, s - 1, False))
            if s < SHORT:
                go(along(k, s, False))
        for j in js:
            put(k, j)
        if s == LONG:
            here = pl.ds(k * CW, CW)
            out(gw.at[here], gw_out.at[here], k)

    def tokens_grad():
        for d in range(1, NF):
            frm = fdev(NF - d)
            rcopy(own.at[frm], own.at[frm], sg_s.at[d - 1], sg_r.at[d - 1], (dp, frm)).wait_recv()
        hot_s = hot[:, :SLOTS]
        for f in range(NF):
            gt[:, f * W:(f + 1) * W] = dot(hot_s, own[f], 1, 0).astype(bf16)
        out(gt, gt_out, CH)

    z_at = LONG + 3
    in_at = z_at + 3
    for t in range(CH + in_at + LONG):
        for s in range(LONG, 0, -1):
            if 0 <= t - in_at - s < CH:
                y_step(t - in_at - s, s)
        if 0 <= t - in_at < CH:
            z_in(t - in_at)
        if 0 <= t - z_at < CH:
            z_sum(t - z_at)
        if t < CH:
            product(t)
        for s in range(LONG, 0, -1):
            if 0 <= t - s < CH:
                ring_step(t - s, s)
        if t == 1:
            ins[2].wait()
            slot_grads()
            z_a, z_i = steps(largest(zb, zb_s, zb_r) * (NF * NY * NZ))
        if t == CH + LONG:
            tokens_grad()

    for d in range(1, NZ):
        rcopy(ered.at[0, pl.ds(0, ZR)], zrecv.at[d - 1], z_s.at[d - 1], z_r.at[d - 1], (dp, fs)).wait_send()
        rcopy(zsum, zrecv.at[d - 1], az_s.at[d - 1], az_r.at[d - 1], (dp, fs)).wait_send()
    for cp in sends:
        cp.wait_send()
    for cp in outs:
        cp.wait()


def shards(tokens, value_grad, value_weight, counts, chosen_rows, loss_scale):
    vmem = pl.BlockSpec(memory_space=pltpu.VMEM)
    hbm, smem = pl.BlockSpec(memory_space=pltpu.HBM), pl.BlockSpec(memory_space=pltpu.SMEM)
    dma = pltpu.SemaphoreType.DMA
    scratch = [
        pltpu.VMEM((ROWS, D), bf16),
        pltpu.VMEM((ROWS, KV), bf16),
        pltpu.VMEM((W, KV), bf16),
        pltpu.VMEM((8, ROWS), jnp.int32),
        pltpu.VMEM((SLOTS, D), bf16),
        pltpu.VMEM((NF, SLOTS, KV), bf16),
        pltpu.VMEM((CH, NF, SLOTS, CW), bf16),
        pltpu.VMEM((NF, SLOTS, W), bf16),
        pltpu.VMEM((NF, SLOTS, W), bf16),
        pltpu.VMEM((NY, W, LANE), f32),
        pltpu.VMEM((CH, LONG, CW, LANE), bf16),
        pltpu.VMEM((CH, SHORT, CW, LANE), bf16),
        pltpu.VMEM((CH, LONG, CW, LANE), bf16),
        pltpu.VMEM((CH, SHORT, CW, LANE), bf16),
        pltpu.VMEM((CH, 3 * ZR, LANE), f32),
        pltpu.VMEM((CH, 3 * ZR, LANE), bf16),
        pltpu.VMEM((NZ - 1, ZR, LANE), bf16),
        pltpu.VMEM((ZR, LANE), bf16),
        pltpu.VMEM((NY, CH, 3 * ZR, LANE), bf16),
        pltpu.VMEM((NF, 8, LANE), f32),
        pltpu.VMEM((NY, 8, LANE), f32),
        pltpu.VMEM((NZ, 8, LANE), f32),
        pltpu.VMEM((ROWS, D), bf16),
        pltpu.VMEM((W, KV), f32),
        dma((3,)), dma((CH + 1,)), dma((NF - 1,)), dma((NF - 1,)), dma((NY - 1,)), dma((NY - 1,)), dma((NZ - 1,)), dma((NZ - 1,)),
        dma((3,)), dma((3,)), dma((4,)), dma((4,)),
        dma((CH, NF - 1)), dma((CH, NF - 1)), dma((NF - 1,)), dma((NF - 1,)),
        dma((CH, LONG)), dma((CH, LONG)), dma((CH, SHORT)), dma((CH, SHORT)),
        dma((NZ - 1,)), dma((NZ - 1,)), dma((NZ - 1,)), dma((NZ - 1,)),
        dma((CH, LONG)), dma((CH, LONG)), dma((CH, SHORT)), dma((CH, SHORT)),
    ]
    return pl.pallas_call(
        kernel,
        out_shape=(
            jax.ShapeDtypeStruct((ROWS, D), bf16),
            jax.ShapeDtypeStruct((W, KV), f32),
        ),
        in_specs=[hbm] * 3 + [smem, vmem, smem],
        out_specs=(hbm, hbm),
        scratch_shapes=scratch,
        compiler_params=pltpu.CompilerParams(
            collective_id=0, has_side_effects=True, vmem_limit_bytes=60 << 20
        ),
    )(tokens, value_grad, value_weight, counts, chosen_rows, loss_scale)


def solution(mesh):
    return jax.shard_map(
        shards,
        mesh=mesh,
        in_specs=(
            P(("dp", "fsdp"), None),
            P(("dp", "fsdp"), None),
            P("fsdp", None),
            P(("dp", "fsdp")),
            P(("dp", "fsdp"), None),
            P(),
        ),
        out_specs=(P(("dp", "fsdp"), None), P("fsdp", None)),
        check_vma=False,
    )
```

```python
import jax
import jax.numpy as jnp
from jax import lax
from jax.experimental import pallas as pl
from jax.experimental.pallas import tpu as pltpu
from jax.sharding import PartitionSpec as P

MESH = pl.DeviceIdType.MESH
NY, NZ, NF = 8, 12, 8
SLOTS = 96
ROWS, D, KV = 128, 4096, 1024
W = D // NF
CH = 4
CW = W // CH
ZR = 48
LANE = KV // NY
LONG, SHORT = NY // 2, NY // 2 - 1
RS_DIRECT, AG_DIRECT = (), (3,)
f32, bf16 = jnp.float32, jnp.bfloat16
TOP, LOW = 2.0 ** 15.4, 2.0 ** -15.4


def dot(a, b, ca, cb):
    return lax.dot_general(a, b, (((ca,), (cb,)), ((), ())), preferred_element_type=f32)


def kernel(
    tok_in, vg_in, wt_in, count, chosen, scale, gt_out, gw_out,
    tok, vg, wt, sel, picked, cots, parts, slot, own, part, el, es, ed, rl, rs, rd, red, ered, zrecv, zsum, full, xb, yb, zb,
    in_s, xb_s, xb_r, yb_s, yb_r, zb_s, zb_r, cot_s, cot_r, sib_s, sib_r, pk_s, pk_r, sg_s, sg_r,
    l_s, l_r, s_s, s_r, z_s, z_r, az_s, az_r, al_s, al_r, as_s, as_r, d_s, d_r, g_s, g_r,
):
    dp, fs = lax.axis_index("dp"), lax.axis_index("fsdp")
    y, z = dp // NZ, lax.rem(dp, NZ)
    c, x = lax.rem(fs, 2), fs // 2
    sgn = 1 - 2 * c
    sib = x * 2 + 1 - c

    def at_y(v):
        return lax.rem(v + 2 * NY, NY)

    ins = [pltpu.make_async_copy(a, b, in_s.at[i]) for i, (a, b) in enumerate(((vg_in, vg), (tok_in, tok), (wt_in, wt)))]
    for cp in ins:
        cp.start()

    y_up, y_dn = at_y(y + sgn) * NZ + z, at_y(y - sgn) * NZ + z

    def zdev(d):
        return lax.rem(z + d, NZ)

    def ydev(d):
        return at_y(y + d) * NZ + z

    def fdev(d):
        return lax.rem(fs + d, NF)

    def xdev(d):
        return lax.rem(x + d, 4) * 2 + c

    def rcopy(src, dst, ss, rs_, dev):
        return pltpu.make_async_remote_copy(
            src_ref=src, dst_ref=dst, send_sem=ss, recv_sem=rs_, device_id=dev, device_id_type=MESH
        )

    barrier = pltpu.get_barrier_semaphore()
    peers = [(dp, fdev(d)) for d in range(1, NF)]
    peers += [(ydev(d), fs) for d in range(1, NY)]
    peers += [(y * NZ + zdev(d), fs) for d in range(1, NZ)]
    for peer in peers:
        pl.semaphore_signal(barrier, inc=1, device_id=peer, device_id_type=MESH)

    n = chosen.shape[1]
    sel[...] = jnp.full(sel.shape, -1, jnp.int32)
    live = lax.broadcasted_iota(jnp.int32, (1, n), 1) < count[0]
    sel[0:1, 0:n] = jnp.where(live, chosen[...], -1)
    rows = lax.broadcasted_iota(jnp.int32, (ROWS, ROWS), 0)
    hot = jnp.where(rows == sel[0:1, :], 1.0, 0.0).astype(bf16)

    def widest(v):
        t = jnp.sum(v * v, axis=0, keepdims=True)
        return jnp.max(t, axis=1, keepdims=True)

    ins[0].wait()
    v = dot(hot, vg[...], 0, 0)[:SLOTS]
    cots[fs] = v.astype(bf16)
    g_sq = widest(v)
    ins[1].wait()
    t_sq = jnp.zeros((1, 1), f32)
    for b in range(4):
        cols = slice(b * 1024, (b + 1) * 1024)
        v = dot(hot, tok[:, cols], 0, 0)[:SLOTS]
        picked[:, cols] = v.astype(bf16)
        t_sq = jnp.maximum(t_sq, widest(v))
    xb[0] = jnp.broadcast_to(jnp.sqrt(t_sq) * jnp.sqrt(g_sq), xb.shape[1:])
    pl.semaphore_wait(barrier, len(peers))

    sends = []

    def go(cp):
        cp.start()
        sends.append(cp)

    def bounds(buf, ss, rs_, devs):
        for d, dev in enumerate(devs):
            go(rcopy(buf.at[0], buf.at[d + 1], ss.at[d], rs_.at[d], dev))

    def largest(buf, ss, rs_):
        top = buf[0]
        for d in range(buf.shape[0] - 1):
            rcopy(buf.at[d + 1], buf.at[d + 1], ss.at[d], rs_.at[d], (dp, fs)).wait_recv()
            top = jnp.maximum(top, buf[d + 1])
        return top

    bounds(xb, xb_s, xb_r, [(dp, fdev(d)) for d in range(1, NF)])

    fwd, back = xdev(sgn + 4), xdev(4 - sgn)
    across = xdev(2)
    mine = cots.at[fs]
    go(rcopy(mine, mine, cot_s.at[0], cot_r.at[0], (dp, fwd)))
    go(rcopy(mine, mine, cot_s.at[1], cot_r.at[1], (dp, back)))
    go(rcopy(mine, mine, sib_s.at[0], sib_r.at[0], (dp, sib)))

    def cot_in(i, frm):
        ref = cots.at[frm]
        rcopy(ref, ref, cot_s.at[i], cot_r.at[i], (dp, frm)).wait_recv()
        if i == 0:
            go(rcopy(ref, ref, cot_s.at[2], cot_r.at[2], (dp, fwd)))
        go(rcopy(ref, ref, sib_s.at[i + 1], sib_r.at[i + 1], (dp, sib)))

    def picks(k):
        for d in (2, 6, 3, 7, 4, 5, 1):
            to = fdev(d)
            cols = pl.ds(pl.multiple_of(to * W + k * CW, CW), CW)
            go(rcopy(picked.at[:, cols], parts.at[k, fs], pk_s.at[k, d - 1], pk_r.at[k, d - 1], (dp, to)))
        cols = pl.ds(pl.multiple_of(fs * W + k * CW, CW), CW)
        parts[k, fs] = picked[:, cols]

    picks(0)
    cot_in(0, back)
    picks(1)

    yb[0] = largest(xb, xb_s, xb_r)
    bounds(yb, yb_s, yb_r, [(ydev(d), fs) for d in range(1, NY)])

    cot_in(1, fwd)
    cot_in(2, across)
    for i, v in enumerate((0, sgn, -sgn, 2)):
        ref = cots.at[lax.rem(x + v + 4, 4) * 2 + 1 - c]
        rcopy(ref, ref, sib_s.at[i], sib_r.at[i], (dp, sib)).wait_recv()

    def steps(bound):
        a = TOP / jnp.maximum(bound[0:1], 1e-30)
        return a, 1.0 / a

    def code(v, a):
        w = LOW + a * jnp.abs(v)
        w = w * w
        w = w * w
        w = w * w
        return jnp.where(v < 0, -w, w).astype(bf16)

    def value(e, i):
        e = e.astype(f32)
        r = lax.rsqrt(lax.rsqrt(jnp.abs(e)))
        w = (r * lax.rsqrt(r) - LOW) * i
        return jnp.where(e < 0, -w, w)

    zb[0] = largest(yb, yb_s, yb_r)
    bounds(zb, zb_s, zb_r, [(y * NZ + zdev(d), fs) for d in range(1, NZ)])
    y_a, y_i = steps(zb[0] * (NF * NY))
    z_a = z_i = None

    def long_copy(k, s):
        src = el.at[k, s]
        return rcopy(src, rl.at[k, s], l_s.at[k, s], l_r.at[k, s], (y_dn, fs))

    def short_copy(k, s):
        src = es.at[k, s]
        return rcopy(src, rs.at[k, s], s_s.at[k, s], s_r.at[k, s], (y_up, fs))

    def direct_copy(k, d):
        return rcopy(ed.at[k, d - 1], rd.at[k, d - 1], d_s.at[k, d - 1], d_r.at[k, d - 1], (ydev(d), fs))

    def product(k):
        for d in range(1, NF):
            frm = fdev(NF - d)
            rcopy(parts.at[k, frm], parts.at[k, frm], pk_s.at[k, d - 1], pk_r.at[k, d - 1], (dp, frm)).wait_recv()
        if k + 2 < CH:
            picks(k + 2)
        a = parts[k].reshape(NF * SLOTS, CW)
        b = cots[...].reshape(NF * SLOTS, KV)
        p = dot(a, b, 0, 0)
        for j in range(NY):
            part[j, k * CW:(k + 1) * CW] = p[:, j * LANE:(j + 1) * LANE]
        here = pl.ds(k * CW, CW)
        if k in RS_DIRECT:
            for d in (4, 3, 5, 2, 6, 1, 7):
                ed[k, d - 1] = code(part[at_y(y + d), here], y_a)
                go(direct_copy(k, d))
            return
        el[k, 0] = code(part[at_y(y - sgn * LONG), here], y_a)
        go(long_copy(k, 0))
        es[k, 0] = code(part[at_y(y + sgn * SHORT), here], y_a)
        go(short_copy(k, 0))

    def reduced(k, total):
        red[k, 0:CW] = total
        ered[k, 0:CW] = code(total, z_a)
        for r in range(3):
            to = 3 * k + r
            d = lax.rem(to - z + NZ, NZ)

            @pl.when(to != z)
            def _():
                src = ered.at[k, pl.ds(r * ZR, ZR)]
                rcopy(src, zrecv.at[d - 1], z_s.at[d - 1], z_r.at[d - 1], (y * NZ + to, fs)).start()

    def ring_step(k, s):
        here = pl.ds(k * CW, CW)
        if k in RS_DIRECT:
            if s == LONG - 1:
                for d in range(1, NY):
                    direct_copy(k, d).wait_recv()
                reduced(k, part[y, here] + jnp.sum(value(rd[k], y_i), axis=0))
            return
        long_copy(k, s - 1).wait_recv()
        if s < LONG:
            el[k, s] = code(part[at_y(y - sgn * (LONG - s)), here] + value(rl[k, s - 1], y_i), y_a)
            go(long_copy(k, s))
        if s <= SHORT:
            short_copy(k, s - 1).wait_recv()
        if s < SHORT:
            es[k, s] = code(part[at_y(y + sgn * (SHORT - s)), here] + value(rs[k, s - 1], y_i), y_a)
            go(short_copy(k, s))
        if s == LONG:
            reduced(k, part[y, here] + value(rl[k, LONG - 1], y_i) + value(rs[k, SHORT - 1], y_i))

    red[:, CW:] = jnp.zeros((CH, 3 * ZR - CW, LANE), f32)
    ered[:, CW:] = jnp.ones((CH, 3 * ZR - CW, LANE), bf16)

    def slot_grads():
        for g in range(2):
            b = cots[g * 4:(g + 1) * 4].reshape(4 * SLOTS, KV)
            q = dot(b, wt[...], 1, 1).astype(bf16)
            slot[g * 4:(g + 1) * 4] = q.reshape(4, SLOTS, W)
        for d in (2, 6, 3, 7, 4, 5, 1):
            to = fdev(d)
            go(rcopy(slot.at[to], own.at[fs], sg_s.at[d - 1], sg_r.at[d - 1], (dp, to)))
        own[fs] = slot[fs]

    def z_sum(k):
        @pl.when(z // 3 == k)
        def _():
            part_z = pl.ds(pl.multiple_of(lax.rem(z, 3) * ZR, 16), ZR)
            for d in range(1, NZ):
                rcopy(zrecv.at[d - 1], zrecv.at[d - 1], z_s.at[d - 1], z_r.at[d - 1], (dp, fs)).wait_recv()
            zsum[...] = code(red[k, part_z] + jnp.sum(value(zrecv[...], z_i), axis=0), z_a)
            for d in (6, 5, 7, 4, 8, 3, 9, 2, 10, 1, 11):
                rcopy(zsum, full.at[y, k, part_z], az_s.at[d - 1], az_r.at[d - 1], (y * NZ + zdev(d), fs)).start()
            full[y, k, part_z] = zsum[...]

    def along(k, s, up):
        ref = full.at[at_y(y - sgn * s) if up else at_y(y + sgn * s), k, pl.ds(0, CW)]
        if up:
            return rcopy(ref, ref, al_s.at[k, s], al_r.at[k, s], (y_up, fs))
        return rcopy(ref, ref, as_s.at[k, s], as_r.at[k, s], (y_dn, fs))

    def arrived(k, s, up):
        j = at_y(y - sgn * (s + 1)) if up else at_y(y + sgn * (s + 1))
        ref = full.at[j, k, pl.ds(0, CW)]
        sems = (al_s.at[k, s], al_r.at[k, s]) if up else (as_s.at[k, s], as_r.at[k, s])
        rcopy(ref, ref, *sems, (dp, fs)).wait_recv()
        return j

    def put(k, j):
        gw_out[k * CW:(k + 1) * CW, pl.ds(pl.multiple_of(j * LANE, LANE), LANE)] = value(full[j, k, 0:CW], z_i / scale[0])

    def gather_copy(k, j, d):
        ref = full.at[j, k, pl.ds(0, CW)]
        return rcopy(ref, ref, g_s.at[k, d - 1], g_r.at[k, d - 1], (ydev(d), fs))

    def z_in(k):
        for r in range(3):
            frm = 3 * k + r
            d = lax.rem(z - frm + NZ, NZ)

            @pl.when(frm != z)
            def _():
                ref = full.at[y, k, pl.ds(r * ZR, ZR)]
                rcopy(ref, ref, az_s.at[d - 1], az_r.at[d - 1], (dp, fs)).wait_recv()
        if k in AG_DIRECT:
            for d in (4, 3, 5, 2, 6, 1, 7):
                go(gather_copy(k, y, d))
        else:
            go(along(k, 0, True))
            go(along(k, 0, False))
        put(k, y)

    def y_step(k, s):
        if k in AG_DIRECT:
            if s == LONG:
                for d in (1, 7, 2, 6, 3, 5, 4):
                    j = at_y(y - d)
                    gather_copy(k, j, d).wait_recv()
                    put(k, j)
            return
        js = [arrived(k, s - 1, True)]
        if s < LONG:
            go(along(k, s, True))
        if s <= SHORT:
            js.append(arrived(k, s - 1, False))
            if s < SHORT:
                go(along(k, s, False))
        for j in js:
            put(k, j)

    def tokens_grad():
        for d in range(1, NF):
            frm = fdev(NF - d)
            rcopy(own.at[frm], own.at[frm], sg_s.at[d - 1], sg_r.at[d - 1], (dp, frm)).wait_recv()
        hot_s = hot[:, :SLOTS]
        for f in range(NF):
            gt_out[:, f * W:(f + 1) * W] = dot(hot_s, own[f], 1, 0).astype(bf16)

    z_at = LONG + 3
    in_at = z_at + 3
    for t in range(CH + in_at + LONG):
        if t < CH:
            product(t)
        for s in range(1, LONG + 1):
            if 0 <= t - s < CH:
                ring_step(t - s, s)
        if 0 <= t - z_at < CH:
            z_sum(t - z_at)
        if 0 <= t - in_at < CH:
            z_in(t - in_at)
        for s in range(1, LONG + 1):
            if 0 <= t - in_at - s < CH:
                y_step(t - in_at - s, s)
        if t == CH - 1:
            ins[2].wait()
            slot_grads()
        if t == 1:
            z_a, z_i = steps(largest(zb, zb_s, zb_r) * (NF * NY * NZ))
        if t == in_at + CH - 1:
            tokens_grad()

    for d in range(1, NZ):
        rcopy(ered.at[0, pl.ds(0, ZR)], zrecv.at[d - 1], z_s.at[d - 1], z_r.at[d - 1], (dp, fs)).wait_send()
        rcopy(zsum, zrecv.at[d - 1], az_s.at[d - 1], az_r.at[d - 1], (dp, fs)).wait_send()
    for cp in sends:
        cp.wait_send()

def shards(tokens, value_grad, value_weight, counts, chosen_rows, loss_scale):
    vmem = pl.BlockSpec(memory_space=pltpu.VMEM)
    hbm, smem = pl.BlockSpec(memory_space=pltpu.HBM), pl.BlockSpec(memory_space=pltpu.SMEM)
    dma = pltpu.SemaphoreType.DMA
    scratch = [
        pltpu.VMEM((ROWS, D), bf16),
        pltpu.VMEM((ROWS, KV), bf16),
        pltpu.VMEM((W, KV), bf16),
        pltpu.VMEM((8, ROWS), jnp.int32),
        pltpu.VMEM((SLOTS, D), bf16),
        pltpu.VMEM((NF, SLOTS, KV), bf16),
        pltpu.VMEM((CH, NF, SLOTS, CW), bf16),
        pltpu.VMEM((NF, SLOTS, W), bf16),
        pltpu.VMEM((NF, SLOTS, W), bf16),
        pltpu.VMEM((NY, W, LANE), f32),
        pltpu.VMEM((CH, LONG, CW, LANE), bf16),
        pltpu.VMEM((CH, SHORT, CW, LANE), bf16),
        pltpu.VMEM((CH, NY - 1, CW, LANE), bf16),
        pltpu.VMEM((CH, LONG, CW, LANE), bf16),
        pltpu.VMEM((CH, SHORT, CW, LANE), bf16),
        pltpu.VMEM((CH, NY - 1, CW, LANE), bf16),
        pltpu.VMEM((CH, 3 * ZR, LANE), f32),
        pltpu.VMEM((CH, 3 * ZR, LANE), bf16),
        pltpu.VMEM((NZ - 1, ZR, LANE), bf16),
        pltpu.VMEM((ZR, LANE), bf16),
        pltpu.VMEM((NY, CH, 3 * ZR, LANE), bf16),
        pltpu.VMEM((NF, 8, LANE), f32),
        pltpu.VMEM((NY, 8, LANE), f32),
        pltpu.VMEM((NZ, 8, LANE), f32),
        dma((3,)), dma((NF - 1,)), dma((NF - 1,)), dma((NY - 1,)), dma((NY - 1,)), dma((NZ - 1,)), dma((NZ - 1,)),
        dma((3,)), dma((3,)), dma((4,)), dma((4,)),
        dma((CH, NF - 1)), dma((CH, NF - 1)), dma((NF - 1,)), dma((NF - 1,)),
        dma((CH, LONG)), dma((CH, LONG)), dma((CH, SHORT)), dma((CH, SHORT)),
        dma((NZ - 1,)), dma((NZ - 1,)), dma((NZ - 1,)), dma((NZ - 1,)),
        dma((CH, LONG)), dma((CH, LONG)), dma((CH, SHORT)), dma((CH, SHORT)),
        dma((CH, NY - 1)), dma((CH, NY - 1)), dma((CH, NY - 1)), dma((CH, NY - 1)),
    ]
    return pl.pallas_call(
        kernel,
        out_shape=(
            pltpu.VMEM((ROWS, D), bf16),
            pltpu.VMEM((W, KV), f32),
        ),
        in_specs=[hbm] * 3 + [smem, vmem, smem],
        out_specs=(vmem, vmem),
        scratch_shapes=scratch,
        compiler_params=pltpu.CompilerParams(
            collective_id=0, has_side_effects=True, vmem_limit_bytes=56 << 20
        ),
    )(tokens, value_grad, value_weight, counts, chosen_rows, loss_scale)


def solution(mesh):
    return jax.shard_map(
        shards,
        mesh=mesh,
        in_specs=(
            P(("dp", "fsdp"), None),
            P(("dp", "fsdp"), None),
            P("fsdp", None),
            P(("dp", "fsdp")),
            P(("dp", "fsdp"), None),
            P(),
        ),
        out_specs=(P(("dp", "fsdp"), None), P("fsdp", None)),
        check_vma=False,
    )
```

```python
import jax
import jax.numpy as jnp
from jax import lax
from jax.experimental import pallas as pl
from jax.experimental.pallas import tpu as pltpu
from jax.sharding import PartitionSpec as P

MESH = pl.DeviceIdType.MESH
NY, NZ, NF = 8, 12, 8
SLOTS = 96
ROWS, D, KV = 128, 4096, 1024
W = D // NF
CH = 4
CW = W // CH
ZR = 48
LANE = KV // NY
LONG, SHORT = NY // 2, NY // 2 - 1
RS_DIRECT, AG_DIRECT = (), (3,)
f32, bf16 = jnp.float32, jnp.bfloat16
TOP, LOW = 2.0 ** 15.4, 2.0 ** -15.4


def dot(a, b, ca, cb):
    return lax.dot_general(a, b, (((ca,), (cb,)), ((), ())), preferred_element_type=f32)


def kernel(
    tok_in, vg_in, wt_in, count, chosen, scale, gt_out, gw_out,
    tok, vg, wt, sel, picked, cots, parts, slot, own, part, el, es, ed, rl, rs, rd, red, ered, zrecv, zsum, full, xb, yb, zb,
    in_s, xb_s, xb_r, yb_s, yb_r, zb_s, zb_r, cot_s, cot_r, sib_s, sib_r, pk_s, pk_r, sg_s, sg_r,
    l_s, l_r, s_s, s_r, z_s, z_r, az_s, az_r, al_s, al_r, as_s, as_r, d_s, d_r, g_s, g_r,
):
    dp, fs = lax.axis_index("dp"), lax.axis_index("fsdp")
    y, z = dp // NZ, lax.rem(dp, NZ)
    c, x = lax.rem(fs, 2), fs // 2
    sgn = 1 - 2 * c
    sib = x * 2 + 1 - c

    def at_y(v):
        return lax.rem(v + 2 * NY, NY)

    ins = [pltpu.make_async_copy(a, b, in_s.at[i]) for i, (a, b) in enumerate(((vg_in, vg), (tok_in, tok), (wt_in, wt)))]
    for cp in ins:
        cp.start()

    y_up, y_dn = at_y(y + sgn) * NZ + z, at_y(y - sgn) * NZ + z

    def zdev(d):
        return lax.rem(z + d, NZ)

    def ydev(d):
        return at_y(y + d) * NZ + z

    def fdev(d):
        return lax.rem(fs + d, NF)

    def xdev(d):
        return lax.rem(x + d, 4) * 2 + c

    def rcopy(src, dst, ss, rs_, dev):
        return pltpu.make_async_remote_copy(
            src_ref=src, dst_ref=dst, send_sem=ss, recv_sem=rs_, device_id=dev, device_id_type=MESH
        )

    barrier = pltpu.get_barrier_semaphore()
    peers = [(dp, fdev(d)) for d in range(1, NF)]
    peers += [(ydev(d), fs) for d in range(1, NY)]
    peers += [(y * NZ + zdev(d), fs) for d in range(1, NZ)]
    for peer in peers:
        pl.semaphore_signal(barrier, inc=1, device_id=peer, device_id_type=MESH)

    n = chosen.shape[1]
    sel[...] = jnp.full(sel.shape, -1, jnp.int32)
    live = lax.broadcasted_iota(jnp.int32, (1, n), 1) < count[0]
    sel[0:1, 0:n] = jnp.where(live, chosen[...], -1)
    rows = lax.broadcasted_iota(jnp.int32, (ROWS, ROWS), 0)
    hot = jnp.where(rows == sel[0:1, :], 1.0, 0.0).astype(bf16)

    def widest(v):
        t = jnp.sum(v * v, axis=0, keepdims=True)
        return jnp.max(t, axis=1, keepdims=True)

    ins[0].wait()
    v = dot(hot, vg[...], 0, 0)[:SLOTS]
    cots[fs] = v.astype(bf16)
    g_sq = widest(v)
    ins[1].wait()
    t_sq = jnp.zeros((1, 1), f32)
    for b in range(4):
        cols = slice(b * 1024, (b + 1) * 1024)
        v = dot(hot, tok[:, cols], 0, 0)[:SLOTS]
        picked[:, cols] = v.astype(bf16)
        t_sq = jnp.maximum(t_sq, widest(v))
    xb[0] = jnp.broadcast_to(jnp.sqrt(t_sq) * jnp.sqrt(g_sq), xb.shape[1:])
    pl.semaphore_wait(barrier, len(peers))

    sends = []

    def go(cp):
        cp.start()
        sends.append(cp)

    def bounds(buf, ss, rs_, devs):
        for d, dev in enumerate(devs):
            go(rcopy(buf.at[0], buf.at[d + 1], ss.at[d], rs_.at[d], dev))

    def largest(buf, ss, rs_):
        top = buf[0]
        for d in range(buf.shape[0] - 1):
            rcopy(buf.at[d + 1], buf.at[d + 1], ss.at[d], rs_.at[d], (dp, fs)).wait_recv()
            top = jnp.maximum(top, buf[d + 1])
        return top

    bounds(xb, xb_s, xb_r, [(dp, fdev(d)) for d in range(1, NF)])

    fwd, back = xdev(sgn + 4), xdev(4 - sgn)
    across = xdev(2)
    mine = cots.at[fs]
    go(rcopy(mine, mine, cot_s.at[0], cot_r.at[0], (dp, fwd)))
    go(rcopy(mine, mine, cot_s.at[1], cot_r.at[1], (dp, back)))
    go(rcopy(mine, mine, sib_s.at[0], sib_r.at[0], (dp, sib)))

    def cot_in(i, frm):
        ref = cots.at[frm]
        rcopy(ref, ref, cot_s.at[i], cot_r.at[i], (dp, frm)).wait_recv()
        if i == 0:
            go(rcopy(ref, ref, cot_s.at[2], cot_r.at[2], (dp, fwd)))
        go(rcopy(ref, ref, sib_s.at[i + 1], sib_r.at[i + 1], (dp, sib)))

    def picks(k):
        for d in (2, 6, 3, 7, 4, 5, 1):
            to = fdev(d)
            cols = pl.ds(pl.multiple_of(to * W + k * CW, CW), CW)
            go(rcopy(picked.at[:, cols], parts.at[k, fs], pk_s.at[k, d - 1], pk_r.at[k, d - 1], (dp, to)))
        cols = pl.ds(pl.multiple_of(fs * W + k * CW, CW), CW)
        parts[k, fs] = picked[:, cols]

    cot_in(0, back)
    picks(0)

    yb[0] = largest(xb, xb_s, xb_r)
    bounds(yb, yb_s, yb_r, [(ydev(d), fs) for d in range(1, NY)])

    cot_in(1, fwd)
    cot_in(2, across)
    picks(1)
    for i, v in enumerate((0, sgn, -sgn, 2)):
        ref = cots.at[lax.rem(x + v + 4, 4) * 2 + 1 - c]
        rcopy(ref, ref, sib_s.at[i], sib_r.at[i], (dp, sib)).wait_recv()

    def steps(bound):
        a = TOP / jnp.maximum(bound[0:1], 1e-30)
        return a, 1.0 / a

    def code(v, a):
        w = LOW + a * jnp.abs(v)
        w = w * w
        w = w * w
        w = w * w
        return jnp.where(v < 0, -w, w).astype(bf16)

    def value(e, i):
        e = e.astype(f32)
        r = lax.rsqrt(lax.rsqrt(jnp.abs(e)))
        w = (r * lax.rsqrt(r) - LOW) * i
        return jnp.where(e < 0, -w, w)

    zb[0] = largest(yb, yb_s, yb_r)
    bounds(zb, zb_s, zb_r, [(y * NZ + zdev(d), fs) for d in range(1, NZ)])
    y_a, y_i = steps(zb[0] * (NF * NY))
    z_a = z_i = None

    def long_copy(k, s):
        src = el.at[k, s]
        return rcopy(src, rl.at[k, s], l_s.at[k, s], l_r.at[k, s], (y_dn, fs))

    def short_copy(k, s):
        src = es.at[k, s]
        return rcopy(src, rs.at[k, s], s_s.at[k, s], s_r.at[k, s], (y_up, fs))

    def direct_copy(k, d):
        return rcopy(ed.at[k, d - 1], rd.at[k, d - 1], d_s.at[k, d - 1], d_r.at[k, d - 1], (ydev(d), fs))

    def product(k):
        for d in range(1, NF):
            frm = fdev(NF - d)
            rcopy(parts.at[k, frm], parts.at[k, frm], pk_s.at[k, d - 1], pk_r.at[k, d - 1], (dp, frm)).wait_recv()
        if k + 2 < CH:
            picks(k + 2)
        a = parts[k].reshape(NF * SLOTS, CW)
        b = cots[...].reshape(NF * SLOTS, KV)
        p = dot(a, b, 0, 0)
        for j in range(NY):
            part[j, k * CW:(k + 1) * CW] = p[:, j * LANE:(j + 1) * LANE]
        here = pl.ds(k * CW, CW)
        if k in RS_DIRECT:
            for d in (4, 3, 5, 2, 6, 1, 7):
                ed[k, d - 1] = code(part[at_y(y + d), here], y_a)
                go(direct_copy(k, d))
            return
        el[k, 0] = code(part[at_y(y - sgn * LONG), here], y_a)
        go(long_copy(k, 0))
        es[k, 0] = code(part[at_y(y + sgn * SHORT), here], y_a)
        go(short_copy(k, 0))

    def reduced(k, total):
        red[k, 0:CW] = total
        ered[k, 0:CW] = code(total, z_a)
        for r in range(3):
            to = 3 * k + r
            d = lax.rem(to - z + NZ, NZ)

            @pl.when(to != z)
            def _():
                src = ered.at[k, pl.ds(r * ZR, ZR)]
                rcopy(src, zrecv.at[d - 1], z_s.at[d - 1], z_r.at[d - 1], (y * NZ + to, fs)).start()

    def ring_step(k, s):
        here = pl.ds(k * CW, CW)
        if k in RS_DIRECT:
            if s == LONG - 1:
                for d in range(1, NY):
                    direct_copy(k, d).wait_recv()
                reduced(k, part[y, here] + jnp.sum(value(rd[k], y_i), axis=0))
            return
        long_copy(k, s - 1).wait_recv()
        if s < LONG:
            el[k, s] = code(part[at_y(y - sgn * (LONG - s)), here] + value(rl[k, s - 1], y_i), y_a)
            go(long_copy(k, s))
        if s <= SHORT:
            short_copy(k, s - 1).wait_recv()
        if s < SHORT:
            es[k, s] = code(part[at_y(y + sgn * (SHORT - s)), here] + value(rs[k, s - 1], y_i), y_a)
            go(short_copy(k, s))
        if s == LONG:
            reduced(k, part[y, here] + value(rl[k, LONG - 1], y_i) + value(rs[k, SHORT - 1], y_i))

    red[:, CW:] = jnp.zeros((CH, 3 * ZR - CW, LANE), f32)
    ered[:, CW:] = jnp.ones((CH, 3 * ZR - CW, LANE), bf16)

    def slot_grads():
        for g in range(2):
            b = cots[g * 4:(g + 1) * 4].reshape(4 * SLOTS, KV)
            q = dot(b, wt[...], 1, 1).astype(bf16)
            slot[g * 4:(g + 1) * 4] = q.reshape(4, SLOTS, W)
        for d in (2, 6, 3, 7, 4, 5, 1):
            to = fdev(d)
            go(rcopy(slot.at[to], own.at[fs], sg_s.at[d - 1], sg_r.at[d - 1], (dp, to)))
        own[fs] = slot[fs]

    def z_sum(k):
        @pl.when(z // 3 == k)
        def _():
            part_z = pl.ds(pl.multiple_of(lax.rem(z, 3) * ZR, 16), ZR)
            for d in range(1, NZ):
                rcopy(zrecv.at[d - 1], zrecv.at[d - 1], z_s.at[d - 1], z_r.at[d - 1], (dp, fs)).wait_recv()
            zsum[...] = code(red[k, part_z] + jnp.sum(value(zrecv[...], z_i), axis=0), z_a)
            for d in (6, 5, 7, 4, 8, 3, 9, 2, 10, 1, 11):
                rcopy(zsum, full.at[y, k, part_z], az_s.at[d - 1], az_r.at[d - 1], (y * NZ + zdev(d), fs)).start()
            full[y, k, part_z] = zsum[...]

    def along(k, s, up):
        ref = full.at[at_y(y - sgn * s) if up else at_y(y + sgn * s), k, pl.ds(0, CW)]
        if up:
            return rcopy(ref, ref, al_s.at[k, s], al_r.at[k, s], (y_up, fs))
        return rcopy(ref, ref, as_s.at[k, s], as_r.at[k, s], (y_dn, fs))

    def arrived(k, s, up):
        j = at_y(y - sgn * (s + 1)) if up else at_y(y + sgn * (s + 1))
        ref = full.at[j, k, pl.ds(0, CW)]
        sems = (al_s.at[k, s], al_r.at[k, s]) if up else (as_s.at[k, s], as_r.at[k, s])
        rcopy(ref, ref, *sems, (dp, fs)).wait_recv()
        return j

    def put(k, j):
        gw_out[k * CW:(k + 1) * CW, pl.ds(pl.multiple_of(j * LANE, LANE), LANE)] = value(full[j, k, 0:CW], z_i / scale[0])

    def gather_copy(k, j, d):
        ref = full.at[j, k, pl.ds(0, CW)]
        return rcopy(ref, ref, g_s.at[k, d - 1], g_r.at[k, d - 1], (ydev(d), fs))

    def z_in(k):
        for r in range(3):
            frm = 3 * k + r
            d = lax.rem(z - frm + NZ, NZ)

            @pl.when(frm != z)
            def _():
                ref = full.at[y, k, pl.ds(r * ZR, ZR)]
                rcopy(ref, ref, az_s.at[d - 1], az_r.at[d - 1], (dp, fs)).wait_recv()
        if k in AG_DIRECT:
            for d in (4, 3, 5, 2, 6, 1, 7):
                go(gather_copy(k, y, d))
        else:
            go(along(k, 0, True))
            go(along(k, 0, False))
        put(k, y)

    def y_step(k, s):
        if k in AG_DIRECT:
            if s == LONG:
                for d in (1, 7, 2, 6, 3, 5, 4):
                    j = at_y(y - d)
                    gather_copy(k, j, d).wait_recv()
                    put(k, j)
            return
        js = [arrived(k, s - 1, True)]
        if s < LONG:
            go(along(k, s, True))
        if s <= SHORT:
            js.append(arrived(k, s - 1, False))
            if s < SHORT:
                go(along(k, s, False))
        for j in js:
            put(k, j)

    def tokens_grad():
        for d in range(1, NF):
            frm = fdev(NF - d)
            rcopy(own.at[frm], own.at[frm], sg_s.at[d - 1], sg_r.at[d - 1], (dp, frm)).wait_recv()
        hot_s = hot[:, :SLOTS]
        for f in range(NF):
            gt_out[:, f * W:(f + 1) * W] = dot(hot_s, own[f], 1, 0).astype(bf16)

    z_at = LONG + 3
    in_at = z_at + 3
    for t in range(CH + in_at + LONG):
        if t < CH:
            product(t)
        for s in range(1, LONG + 1):
            if 0 <= t - s < CH:
                ring_step(t - s, s)
        if 0 <= t - z_at < CH:
            z_sum(t - z_at)
        if 0 <= t - in_at < CH:
            z_in(t - in_at)
        for s in range(1, LONG + 1):
            if 0 <= t - in_at - s < CH:
                y_step(t - in_at - s, s)
        if t == CH - 1:
            ins[2].wait()
            slot_grads()
        if t == 1:
            z_a, z_i = steps(largest(zb, zb_s, zb_r) * (NF * NY * NZ))
        if t == in_at + CH - 1:
            tokens_grad()

    for d in range(1, NZ):
        rcopy(ered.at[0, pl.ds(0, ZR)], zrecv.at[d - 1], z_s.at[d - 1], z_r.at[d - 1], (dp, fs)).wait_send()
        rcopy(zsum, zrecv.at[d - 1], az_s.at[d - 1], az_r.at[d - 1], (dp, fs)).wait_send()
    for cp in sends:
        cp.wait_send()

def shards(tokens, value_grad, value_weight, counts, chosen_rows, loss_scale):
    vmem = pl.BlockSpec(memory_space=pltpu.VMEM)
    hbm, smem = pl.BlockSpec(memory_space=pltpu.HBM), pl.BlockSpec(memory_space=pltpu.SMEM)
    dma = pltpu.SemaphoreType.DMA
    scratch = [
        pltpu.VMEM((ROWS, D), bf16),
        pltpu.VMEM((ROWS, KV), bf16),
        pltpu.VMEM((W, KV), bf16),
        pltpu.VMEM((8, ROWS), jnp.int32),
        pltpu.VMEM((SLOTS, D), bf16),
        pltpu.VMEM((NF, SLOTS, KV), bf16),
        pltpu.VMEM((CH, NF, SLOTS, CW), bf16),
        pltpu.VMEM((NF, SLOTS, W), bf16),
        pltpu.VMEM((NF, SLOTS, W), bf16),
        pltpu.VMEM((NY, W, LANE), f32),
        pltpu.VMEM((CH, LONG, CW, LANE), bf16),
        pltpu.VMEM((CH, SHORT, CW, LANE), bf16),
        pltpu.VMEM((CH, NY - 1, CW, LANE), bf16),
        pltpu.VMEM((CH, LONG, CW, LANE), bf16),
        pltpu.VMEM((CH, SHORT, CW, LANE), bf16),
        pltpu.VMEM((CH, NY - 1, CW, LANE), bf16),
        pltpu.VMEM((CH, 3 * ZR, LANE), f32),
        pltpu.VMEM((CH, 3 * ZR, LANE), bf16),
        pltpu.VMEM((NZ - 1, ZR, LANE), bf16),
        pltpu.VMEM((ZR, LANE), bf16),
        pltpu.VMEM((NY, CH, 3 * ZR, LANE), bf16),
        pltpu.VMEM((NF, 8, LANE), f32),
        pltpu.VMEM((NY, 8, LANE), f32),
        pltpu.VMEM((NZ, 8, LANE), f32),
        dma((3,)), dma((NF - 1,)), dma((NF - 1,)), dma((NY - 1,)), dma((NY - 1,)), dma((NZ - 1,)), dma((NZ - 1,)),
        dma((3,)), dma((3,)), dma((4,)), dma((4,)),
        dma((CH, NF - 1)), dma((CH, NF - 1)), dma((NF - 1,)), dma((NF - 1,)),
        dma((CH, LONG)), dma((CH, LONG)), dma((CH, SHORT)), dma((CH, SHORT)),
        dma((NZ - 1,)), dma((NZ - 1,)), dma((NZ - 1,)), dma((NZ - 1,)),
        dma((CH, LONG)), dma((CH, LONG)), dma((CH, SHORT)), dma((CH, SHORT)),
        dma((CH, NY - 1)), dma((CH, NY - 1)), dma((CH, NY - 1)), dma((CH, NY - 1)),
    ]
    return pl.pallas_call(
        kernel,
        out_shape=(
            pltpu.VMEM((ROWS, D), bf16),
            pltpu.VMEM((W, KV), f32),
        ),
        in_specs=[hbm] * 3 + [smem, vmem, smem],
        out_specs=(vmem, vmem),
        scratch_shapes=scratch,
        compiler_params=pltpu.CompilerParams(
            collective_id=0, has_side_effects=True, vmem_limit_bytes=56 << 20
        ),
    )(tokens, value_grad, value_weight, counts, chosen_rows, loss_scale)


def solution(mesh):
    return jax.shard_map(
        shards,
        mesh=mesh,
        in_specs=(
            P(("dp", "fsdp"), None),
            P(("dp", "fsdp"), None),
            P("fsdp", None),
            P(("dp", "fsdp")),
            P(("dp", "fsdp"), None),
            P(),
        ),
        out_specs=(P(("dp", "fsdp"), None), P("fsdp", None)),
        check_vma=False,
    )
```

```python
import jax
import jax.numpy as jnp
from jax import lax
from jax.experimental import pallas as pl
from jax.experimental.pallas import tpu as pltpu
from jax.sharding import PartitionSpec as P

MESH = pl.DeviceIdType.MESH
NY, NZ, NF = 8, 12, 8
SLOTS = 96
ROWS, D, KV = 128, 4096, 1024
W = D // NF
CH = 4
CW = W // CH
ZR = 48
LANE = KV // NY
LONG, SHORT = NY // 2, NY // 2 - 1
RS_DIRECT, AG_DIRECT = (), (3,)
f32, bf16 = jnp.float32, jnp.bfloat16
TOP, LOW = 2.0 ** 15.4, 2.0 ** -15.4


def dot(a, b, ca, cb):
    return lax.dot_general(a, b, (((ca,), (cb,)), ((), ())), preferred_element_type=f32)


def kernel(
    tok_in, vg_in, wt_in, count, chosen, scale, gt_out, gw_out,
    tok, vg, wt, sel, picked, cots, parts, slot, own, part, el, es, ed, rl, rs, rd, red, ered, zrecv, zsum, full, xb, yb, zb,
    in_s, xb_s, xb_r, yb_s, yb_r, zb_s, zb_r, cot_s, cot_r, sib_s, sib_r, pk_s, pk_r, sg_s, sg_r,
    l_s, l_r, s_s, s_r, z_s, z_r, az_s, az_r, al_s, al_r, as_s, as_r, d_s, d_r, g_s, g_r,
):
    dp, fs = lax.axis_index("dp"), lax.axis_index("fsdp")
    y, z = dp // NZ, lax.rem(dp, NZ)
    c, x = lax.rem(fs, 2), fs // 2
    sgn = 1 - 2 * c
    sib = x * 2 + 1 - c

    def at_y(v):
        return lax.rem(v + 2 * NY, NY)

    ins = [pltpu.make_async_copy(a, b, in_s.at[i]) for i, (a, b) in enumerate(((vg_in, vg), (tok_in, tok), (wt_in, wt)))]
    for cp in ins:
        cp.start()

    y_up, y_dn = at_y(y + sgn) * NZ + z, at_y(y - sgn) * NZ + z

    def zdev(d):
        return lax.rem(z + d, NZ)

    def ydev(d):
        return at_y(y + d) * NZ + z

    def fdev(d):
        return lax.rem(fs + d, NF)

    def xdev(d):
        return lax.rem(x + d, 4) * 2 + c

    def rcopy(src, dst, ss, rs_, dev):
        return pltpu.make_async_remote_copy(
            src_ref=src, dst_ref=dst, send_sem=ss, recv_sem=rs_, device_id=dev, device_id_type=MESH
        )

    barrier = pltpu.get_barrier_semaphore()
    peers = [(dp, fdev(d)) for d in range(1, NF)]
    peers += [(ydev(d), fs) for d in range(1, NY)]
    peers += [(y * NZ + zdev(d), fs) for d in range(1, NZ)]
    for peer in peers:
        pl.semaphore_signal(barrier, inc=1, device_id=peer, device_id_type=MESH)

    n = chosen.shape[1]
    sel[...] = jnp.full(sel.shape, -1, jnp.int32)
    live = lax.broadcasted_iota(jnp.int32, (1, n), 1) < count[0]
    sel[0:1, 0:n] = jnp.where(live, chosen[...], -1)
    rows = lax.broadcasted_iota(jnp.int32, (ROWS, ROWS), 0)
    hot = jnp.where(rows == sel[0:1, :], 1.0, 0.0).astype(bf16)

    def widest(v):
        t = jnp.sum(v * v, axis=0, keepdims=True)
        return jnp.max(t, axis=1, keepdims=True)

    ins[0].wait()
    v = dot(hot, vg[...], 0, 0)[:SLOTS]
    cots[fs] = v.astype(bf16)
    g_sq = widest(v)
    ins[1].wait()
    t_sq = jnp.zeros((1, 1), f32)
    for b in range(4):
        cols = slice(b * 1024, (b + 1) * 1024)
        v = dot(hot, tok[:, cols], 0, 0)[:SLOTS]
        picked[:, cols] = v.astype(bf16)
        t_sq = jnp.maximum(t_sq, widest(v))
    xb[0] = jnp.broadcast_to(jnp.sqrt(t_sq) * jnp.sqrt(g_sq), xb.shape[1:])
    pl.semaphore_wait(barrier, len(peers))

    sends = []

    def go(cp):
        cp.start()
        sends.append(cp)

    def bounds(buf, ss, rs_, devs):
        for d, dev in enumerate(devs):
            go(rcopy(buf.at[0], buf.at[d + 1], ss.at[d], rs_.at[d], dev))

    def largest(buf, ss, rs_):
        top = buf[0]
        for d in range(buf.shape[0] - 1):
            rcopy(buf.at[d + 1], buf.at[d + 1], ss.at[d], rs_.at[d], (dp, fs)).wait_recv()
            top = jnp.maximum(top, buf[d + 1])
        return top

    bounds(xb, xb_s, xb_r, [(dp, fdev(d)) for d in range(1, NF)])

    fwd, back = xdev(sgn + 4), xdev(4 - sgn)
    across = xdev(2)
    mine = cots.at[fs]
    go(rcopy(mine, mine, cot_s.at[0], cot_r.at[0], (dp, fwd)))
    go(rcopy(mine, mine, cot_s.at[1], cot_r.at[1], (dp, back)))
    go(rcopy(mine, mine, sib_s.at[0], sib_r.at[0], (dp, sib)))

    def cot_in(i, frm):
        ref = cots.at[frm]
        rcopy(ref, ref, cot_s.at[i], cot_r.at[i], (dp, frm)).wait_recv()
        if i == 0:
            go(rcopy(ref, ref, cot_s.at[2], cot_r.at[2], (dp, fwd)))
        go(rcopy(ref, ref, sib_s.at[i + 1], sib_r.at[i + 1], (dp, sib)))

    def picks(k):
        for d in (4, 3, 5, 2, 6, 1, 7):
            to = fdev(d)
            cols = pl.ds(pl.multiple_of(to * W + k * CW, CW), CW)
            go(rcopy(picked.at[:, cols], parts.at[k, fs], pk_s.at[k, d - 1], pk_r.at[k, d - 1], (dp, to)))
        cols = pl.ds(pl.multiple_of(fs * W + k * CW, CW), CW)
        parts[k, fs] = picked[:, cols]

    cot_in(0, back)
    picks(0)

    yb[0] = largest(xb, xb_s, xb_r)
    bounds(yb, yb_s, yb_r, [(ydev(d), fs) for d in range(1, NY)])

    cot_in(1, fwd)
    cot_in(2, across)
    picks(1)
    for i, v in enumerate((0, sgn, -sgn, 2)):
        ref = cots.at[lax.rem(x + v + 4, 4) * 2 + 1 - c]
        rcopy(ref, ref, sib_s.at[i], sib_r.at[i], (dp, sib)).wait_recv()

    def steps(bound):
        a = TOP / jnp.maximum(bound[0:1], 1e-30)
        return a, 1.0 / a

    def code(v, a):
        w = LOW + a * jnp.abs(v)
        w = w * w
        w = w * w
        w = w * w
        return jnp.where(v < 0, -w, w).astype(bf16)

    def value(e, i):
        e = e.astype(f32)
        r = lax.rsqrt(lax.rsqrt(jnp.abs(e)))
        w = (r * lax.rsqrt(r) - LOW) * i
        return jnp.where(e < 0, -w, w)

    zb[0] = largest(yb, yb_s, yb_r)
    bounds(zb, zb_s, zb_r, [(y * NZ + zdev(d), fs) for d in range(1, NZ)])
    y_a, y_i = steps(zb[0] * (NF * NY))
    z_a = z_i = None

    def long_copy(k, s):
        src = el.at[k, s]
        return rcopy(src, rl.at[k, s], l_s.at[k, s], l_r.at[k, s], (y_dn, fs))

    def short_copy(k, s):
        src = es.at[k, s]
        return rcopy(src, rs.at[k, s], s_s.at[k, s], s_r.at[k, s], (y_up, fs))

    def direct_copy(k, d):
        return rcopy(ed.at[k, d - 1], rd.at[k, d - 1], d_s.at[k, d - 1], d_r.at[k, d - 1], (ydev(d), fs))

    def product(k):
        for d in range(1, NF):
            frm = fdev(NF - d)
            rcopy(parts.at[k, frm], parts.at[k, frm], pk_s.at[k, d - 1], pk_r.at[k, d - 1], (dp, frm)).wait_recv()
        if k + 2 < CH:
            picks(k + 2)
        a = parts[k].reshape(NF * SLOTS, CW)
        b = cots[...].reshape(NF * SLOTS, KV)
        p = dot(a, b, 0, 0)
        for j in range(NY):
            part[j, k * CW:(k + 1) * CW] = p[:, j * LANE:(j + 1) * LANE]
        here = pl.ds(k * CW, CW)
        if k in RS_DIRECT:
            for d in (4, 3, 5, 2, 6, 1, 7):
                ed[k, d - 1] = code(part[at_y(y + d), here], y_a)
                go(direct_copy(k, d))
            return
        el[k, 0] = code(part[at_y(y - sgn * LONG), here], y_a)
        go(long_copy(k, 0))
        es[k, 0] = code(part[at_y(y + sgn * SHORT), here], y_a)
        go(short_copy(k, 0))

    def reduced(k, total):
        red[k, 0:CW] = total
        ered[k, 0:CW] = code(total, z_a)
        for r in range(3):
            to = 3 * k + r
            d = lax.rem(to - z + NZ, NZ)

            @pl.when(to != z)
            def _():
                src = ered.at[k, pl.ds(r * ZR, ZR)]
                rcopy(src, zrecv.at[d - 1], z_s.at[d - 1], z_r.at[d - 1], (y * NZ + to, fs)).start()

    def ring_step(k, s):
        here = pl.ds(k * CW, CW)
        if k in RS_DIRECT:
            if s == LONG - 1:
                for d in range(1, NY):
                    direct_copy(k, d).wait_recv()
                reduced(k, part[y, here] + jnp.sum(value(rd[k], y_i), axis=0))
            return
        long_copy(k, s - 1).wait_recv()
        if s < LONG:
            el[k, s] = code(part[at_y(y - sgn * (LONG - s)), here] + value(rl[k, s - 1], y_i), y_a)
            go(long_copy(k, s))
        if s <= SHORT:
            short_copy(k, s - 1).wait_recv()
        if s < SHORT:
            es[k, s] = code(part[at_y(y + sgn * (SHORT - s)), here] + value(rs[k, s - 1], y_i), y_a)
            go(short_copy(k, s))
        if s == LONG:
            reduced(k, part[y, here] + value(rl[k, LONG - 1], y_i) + value(rs[k, SHORT - 1], y_i))

    red[:, CW:] = jnp.zeros((CH, 3 * ZR - CW, LANE), f32)
    ered[:, CW:] = jnp.ones((CH, 3 * ZR - CW, LANE), bf16)

    def slot_grads():
        for g in range(2):
            b = cots[g * 4:(g + 1) * 4].reshape(4 * SLOTS, KV)
            q = dot(b, wt[...], 1, 1).astype(bf16)
            slot[g * 4:(g + 1) * 4] = q.reshape(4, SLOTS, W)
        for d in (4, 3, 5, 2, 6, 1, 7):
            to = fdev(d)
            go(rcopy(slot.at[to], own.at[fs], sg_s.at[d - 1], sg_r.at[d - 1], (dp, to)))
        own[fs] = slot[fs]

    def z_sum(k):
        @pl.when(z // 3 == k)
        def _():
            part_z = pl.ds(pl.multiple_of(lax.rem(z, 3) * ZR, 16), ZR)
            for d in range(1, NZ):
                rcopy(zrecv.at[d - 1], zrecv.at[d - 1], z_s.at[d - 1], z_r.at[d - 1], (dp, fs)).wait_recv()
            zsum[...] = code(red[k, part_z] + jnp.sum(value(zrecv[...], z_i), axis=0), z_a)
            for d in (6, 5, 7, 4, 8, 3, 9, 2, 10, 1, 11):
                rcopy(zsum, full.at[y, k, part_z], az_s.at[d - 1], az_r.at[d - 1], (y * NZ + zdev(d), fs)).start()
            full[y, k, part_z] = zsum[...]

    def along(k, s, up):
        ref = full.at[at_y(y - sgn * s) if up else at_y(y + sgn * s), k, pl.ds(0, CW)]
        if up:
            return rcopy(ref, ref, al_s.at[k, s], al_r.at[k, s], (y_up, fs))
        return rcopy(ref, ref, as_s.at[k, s], as_r.at[k, s], (y_dn, fs))

    def arrived(k, s, up):
        j = at_y(y - sgn * (s + 1)) if up else at_y(y + sgn * (s + 1))
        ref = full.at[j, k, pl.ds(0, CW)]
        sems = (al_s.at[k, s], al_r.at[k, s]) if up else (as_s.at[k, s], as_r.at[k, s])
        rcopy(ref, ref, *sems, (dp, fs)).wait_recv()
        return j

    def put(k, j):
        gw_out[k * CW:(k + 1) * CW, pl.ds(pl.multiple_of(j * LANE, LANE), LANE)] = value(full[j, k, 0:CW], z_i / scale[0])

    def gather_copy(k, j, d):
        ref = full.at[j, k, pl.ds(0, CW)]
        return rcopy(ref, ref, g_s.at[k, d - 1], g_r.at[k, d - 1], (ydev(d), fs))

    def z_in(k):
        for r in range(3):
            frm = 3 * k + r
            d = lax.rem(z - frm + NZ, NZ)

            @pl.when(frm != z)
            def _():
                ref = full.at[y, k, pl.ds(r * ZR, ZR)]
                rcopy(ref, ref, az_s.at[d - 1], az_r.at[d - 1], (dp, fs)).wait_recv()
        if k in AG_DIRECT:
            for d in (4, 3, 5, 2, 6, 1, 7):
                go(gather_copy(k, y, d))
        else:
            go(along(k, 0, True))
            go(along(k, 0, False))
        put(k, y)

    def y_step(k, s):
        if k in AG_DIRECT:
            if s == LONG:
                for d in (1, 7, 2, 6, 3, 5, 4):
                    j = at_y(y - d)
                    gather_copy(k, j, d).wait_recv()
                    put(k, j)
            return
        js = [arrived(k, s - 1, True)]
        if s < LONG:
            go(along(k, s, True))
        if s <= SHORT:
            js.append(arrived(k, s - 1, False))
            if s < SHORT:
                go(along(k, s, False))
        for j in js:
            put(k, j)

    def tokens_grad():
        for d in range(1, NF):
            frm = fdev(NF - d)
            rcopy(own.at[frm], own.at[frm], sg_s.at[d - 1], sg_r.at[d - 1], (dp, frm)).wait_recv()
        hot_s = hot[:, :SLOTS]
        for f in range(NF):
            gt_out[:, f * W:(f + 1) * W] = dot(hot_s, own[f], 1, 0).astype(bf16)

    z_at = LONG + 3
    in_at = z_at + 3
    for t in range(CH + in_at + LONG):
        if t < CH:
            product(t)
        for s in range(1, LONG + 1):
            if 0 <= t - s < CH:
                ring_step(t - s, s)
        if 0 <= t - z_at < CH:
            z_sum(t - z_at)
        if 0 <= t - in_at < CH:
            z_in(t - in_at)
        for s in range(1, LONG + 1):
            if 0 <= t - in_at - s < CH:
                y_step(t - in_at - s, s)
        if t == CH - 1:
            ins[2].wait()
            slot_grads()
        if t == 1:
            z_a, z_i = steps(largest(zb, zb_s, zb_r) * (NF * NY * NZ))
        if t == in_at + CH - 1:
            tokens_grad()

    for d in range(1, NZ):
        rcopy(ered.at[0, pl.ds(0, ZR)], zrecv.at[d - 1], z_s.at[d - 1], z_r.at[d - 1], (dp, fs)).wait_send()
        rcopy(zsum, zrecv.at[d - 1], az_s.at[d - 1], az_r.at[d - 1], (dp, fs)).wait_send()
    for cp in sends:
        cp.wait_send()

def shards(tokens, value_grad, value_weight, counts, chosen_rows, loss_scale):
    vmem = pl.BlockSpec(memory_space=pltpu.VMEM)
    hbm, smem = pl.BlockSpec(memory_space=pltpu.HBM), pl.BlockSpec(memory_space=pltpu.SMEM)
    dma = pltpu.SemaphoreType.DMA
    scratch = [
        pltpu.VMEM((ROWS, D), bf16),
        pltpu.VMEM((ROWS, KV), bf16),
        pltpu.VMEM((W, KV), bf16),
        pltpu.VMEM((8, ROWS), jnp.int32),
        pltpu.VMEM((SLOTS, D), bf16),
        pltpu.VMEM((NF, SLOTS, KV), bf16),
        pltpu.VMEM((CH, NF, SLOTS, CW), bf16),
        pltpu.VMEM((NF, SLOTS, W), bf16),
        pltpu.VMEM((NF, SLOTS, W), bf16),
        pltpu.VMEM((NY, W, LANE), f32),
        pltpu.VMEM((CH, LONG, CW, LANE), bf16),
        pltpu.VMEM((CH, SHORT, CW, LANE), bf16),
        pltpu.VMEM((CH, NY - 1, CW, LANE), bf16),
        pltpu.VMEM((CH, LONG, CW, LANE), bf16),
        pltpu.VMEM((CH, SHORT, CW, LANE), bf16),
        pltpu.VMEM((CH, NY - 1, CW, LANE), bf16),
        pltpu.VMEM((CH, 3 * ZR, LANE), f32),
        pltpu.VMEM((CH, 3 * ZR, LANE), bf16),
        pltpu.VMEM((NZ - 1, ZR, LANE), bf16),
        pltpu.VMEM((ZR, LANE), bf16),
        pltpu.VMEM((NY, CH, 3 * ZR, LANE), bf16),
        pltpu.VMEM((NF, 8, LANE), f32),
        pltpu.VMEM((NY, 8, LANE), f32),
        pltpu.VMEM((NZ, 8, LANE), f32),
        dma((3,)), dma((NF - 1,)), dma((NF - 1,)), dma((NY - 1,)), dma((NY - 1,)), dma((NZ - 1,)), dma((NZ - 1,)),
        dma((3,)), dma((3,)), dma((4,)), dma((4,)),
        dma((CH, NF - 1)), dma((CH, NF - 1)), dma((NF - 1,)), dma((NF - 1,)),
        dma((CH, LONG)), dma((CH, LONG)), dma((CH, SHORT)), dma((CH, SHORT)),
        dma((NZ - 1,)), dma((NZ - 1,)), dma((NZ - 1,)), dma((NZ - 1,)),
        dma((CH, LONG)), dma((CH, LONG)), dma((CH, SHORT)), dma((CH, SHORT)),
        dma((CH, NY - 1)), dma((CH, NY - 1)), dma((CH, NY - 1)), dma((CH, NY - 1)),
    ]
    return pl.pallas_call(
        kernel,
        out_shape=(
            pltpu.VMEM((ROWS, D), bf16),
            pltpu.VMEM((W, KV), f32),
        ),
        in_specs=[hbm] * 3 + [smem, vmem, smem],
        out_specs=(vmem, vmem),
        scratch_shapes=scratch,
        compiler_params=pltpu.CompilerParams(
            collective_id=0, has_side_effects=True, vmem_limit_bytes=56 << 20
        ),
    )(tokens, value_grad, value_weight, counts, chosen_rows, loss_scale)


def solution(mesh):
    return jax.shard_map(
        shards,
        mesh=mesh,
        in_specs=(
            P(("dp", "fsdp"), None),
            P(("dp", "fsdp"), None),
            P("fsdp", None),
            P(("dp", "fsdp")),
            P(("dp", "fsdp"), None),
            P(),
        ),
        out_specs=(P(("dp", "fsdp"), None), P("fsdp", None)),
        check_vma=False,
    )
```
